128 devices in a mesh: ctx: 16 (over y, x_hi, core), fsdp: 8 (over x_lo, z).
Axes of the slice: x: 4 (x_hi: 2, x_lo: 2; x = x_hi * 2 + x_lo), y: 4, z: 4, core: 2. Of those that a mesh axis runs over, the one named last changes fastest.
Arguments:
- tokens: bfloat16 [8, 2048, 1024], P('fsdp', 'ctx'), may hold values from -6 to 6
- block_order: int32 [16], replicated, may hold values from 0 to 15, each once
- routes: int32 [8, 2048, 8], P('fsdp', 'ctx'), may hold values from 0 to 9, all different within a row; in each aligned block of 128 rows (0 to 127, 128 to 255, ..., all dimensions but the last counted through in order) at most 128 rows name the same one
- attn_gain: bfloat16 [1024], P('fsdp'), may hold values from 0.5 to 1.5
- qkv_weight: bfloat16 [1024, 2048], P('fsdp'), may hold values from -0.1875 to 0.1875
- proj_weight: bfloat16 [1024, 1024], P('fsdp'), may hold values from -3 to 3
- moe_gain: bfloat16 [1024], P('fsdp'), may hold values from 0.5 to 1.5
- router_weight: bfloat16 [1024, 10], P('fsdp'), may hold values from -0.09375 to 0.09375
- expert_in: bfloat16 [1024, 10, 1024], P('fsdp'), may hold values from -0.1875 to 0.1875
- expert_down: bfloat16 [1024, 10, 512], P('fsdp'), may hold values from -1 to 1
- cotangent: bfloat16 [8, 2048, 1024], P('fsdp', 'ctx'), may hold values from -6 to 6
Outputs:
- layer_out: bfloat16 [8, 2048, 1024], P('fsdp', 'ctx')
- tokens_grad: float32 [8, 2048, 1024], P('fsdp', 'ctx')
- attn_gain_grad: float32 [1024], P('fsdp')
- qkv_grad: float32 [1024, 2048], P('fsdp')
- proj_grad: float32 [1024, 1024], P('fsdp')
- moe_gain_grad: float32 [1024], P('fsdp')
- router_grad: float32 [1024, 10], P('fsdp')
- expert_in_grad: float32 [1024, 10, 1024], P('fsdp')
- expert_down_grad: float32 [1024, 10, 512], P('fsdp')
The draws below stay inside these ranges and needn't reach their ends.
Inputs may be any that keep to these rules, and one draw needn't show every extreme that they name: `block_order`: a permutation of the indices of ctx. `routes`: each row names 8 different experts; in each device's 128 rows no expert is named more than 128 times, a bound that some block reaches there in some devices' rows.
All inputs are finite; a program needn't handle non-finite values.
Results may differ from the reference program's by a relative error of at most 0.025.
Values may be sent and summed in bfloat16 or wider, within the bound.
No kernel may reach another device: no remote copies, remote signals or barrier semaphores. Data moves between devices by JAX's collectives and lax.ppermute only.
A program may use at most 192 MiB of HBM per device.

```python
import math
import jax
import jax.numpy as jnp
import numpy as np
from jax import lax

D = 1024
HEADS = 16
KV_HEADS = 8
HEAD_DIM = 64
FF = 512
TOPK = 8
EXPERTS = 10
TOK_DEV = 128
CAPACITY = 128
SEQLEN = 2048
SEQS = 8
QKV = 2048
N_CTX = 16


def block_levels(rng, extent, cuts, low, high):
    level = 1.0
    for dim, parts in cuts:
        heights = jax.random.uniform(jax.random.fold_in(jax.random.fold_in(rng, 6), dim), (parts,), jnp.float32, low / len(cuts), high / len(cuts))
        level = level * jnp.repeat(jnp.exp(heights), extent[dim] // parts).reshape((-1,) + (1,) * (len(extent) - 1 - dim))
    return level


def shared_out(stream_key, own, number, rows, number_of, top, bound, slope):
    sequence = jax.random.permutation(stream_key, number_of)
    crowded, common = portions_of(number_of, rows * top, bound, slope, True), portions_of(number_of, rows * top, bound, slope, False)
    places = jnp.arange(number_of)

    def named(sizes, offset_by):
        used = int((sizes > 0).sum())
        fixed = max(1, used // 4)
        shifted = fixed + (places - fixed + offset_by * (used - fixed)) % max(1, number_of - fixed)
        return jnp.zeros((number_of,), jnp.int32).at[sequence[jnp.where(places < fixed, places, shifted)]].set(jnp.asarray(sizes, jnp.int32))

    sizes = jnp.where(number % 4 == 0, named(crowded, number // 4), named(common, number - number // 4 - 1))
    mixed = jax.random.permutation(jax.random.fold_in(own, 3), number_of)
    donor, taker = mixed[0:number_of // 2 * 2:2], mixed[1:number_of // 2 * 2:2]
    room = jnp.minimum(sizes[donor] - 1, bound - sizes[taker]) // 2
    room = jnp.where((donor == sequence[0]) | (taker == sequence[0]) | (sizes[taker] == 0), 0, jnp.maximum(room, 0))
    shifted = jax.random.randint(jax.random.fold_in(own, 4), (number_of // 2,), 0, 1 << 20) % (room + 1)
    sizes = sizes.at[donor].add(-shifted).at[taker].add(shifted)
    members = jnp.searchsorted(jnp.cumsum(sizes), jnp.arange(rows * top), side="right").astype(jnp.int32)
    table = members.reshape(top, rows).T
    table = table[jax.random.permutation(jax.random.fold_in(own, 1), rows)]
    offset_by = jax.random.randint(jax.random.fold_in(own, 2), (rows, 1), 0, top)
    return jnp.take_along_axis(table, (jnp.arange(top)[None, :] + offset_by) % top, axis=1)


def portions_of(number_of, total, limit, slope, full):
    portions = [(1 << 20) // math.isqrt(grade ** slope) + 1 for grade in range(1, number_of + 1)]
    largest = limit if full else min(limit, max(-(-total // number_of), total * portions[0] // sum(portions)))
    least = 1 if total - largest >= number_of - 1 else 0
    counts, surplus = [largest] + [least] * (number_of - 1), total - largest - least * (number_of - 1)
    while surplus > 0:
        free = [i for i in range(1, number_of) if counts[i] < largest] or [i for i in range(1, number_of) if counts[i] < limit]
        whole, budget = sum([portions[i] for i in free]), surplus
        for i in free:
            extra = min(limit - counts[i], max(1, budget * portions[i] // whole), surplus)
            counts[i] = counts[i] + extra
            surplus = surplus - extra
    return np.array(counts)


def noise(stream_key, dims, deviation, reach, cuts=(), kind=jnp.bfloat16):
    loudness = block_levels(stream_key, dims, cuts, -0.22, 0.18) if cuts else 1.0
    drawn = jax.random.normal(stream_key, dims, jnp.float32) * deviation * loudness
    return jnp.minimum(jnp.maximum(drawn, -reach), reach).astype(kind)


def setup_inputs(seed: int = 0) -> dict:
    key_list = jax.random.split(jax.random.key(seed), 12)
    tokens = noise(key_list[0], (SEQS, SEQLEN, D), 1.0, 6.0, ((0, 8), (1, 16)))
    block_order = jax.random.permutation(key_list[1], N_CTX).astype(jnp.int32)
    routes_keys = jax.random.split(jax.random.fold_in(key_list[2], 1), SEQS * SEQLEN // TOK_DEV)
    routes_turns = jax.random.permutation(jax.random.fold_in(key_list[2], 3), SEQS * SEQLEN // TOK_DEV)
    routes = jax.vmap(lambda own, number: shared_out(jax.random.fold_in(key_list[2], 2), own, number, TOK_DEV, EXPERTS, TOPK, CAPACITY, 1))(routes_keys, routes_turns).reshape((SEQS, SEQLEN, TOPK))
    attn_gain = jnp.clip(1.0 + 0.1 * jax.random.normal(key_list[3], (D,), jnp.float32), 0.5, 1.5).astype(jnp.bfloat16)
    qkv_weight = noise(key_list[4], (D, QKV), D ** -0.5, 0.1875, ((0, 8),))
    proj_weight = noise(key_list[5], (D, HEADS * HEAD_DIM), 4 ** -0.5, 3.0, ((0, 8),))
    moe_gain = jnp.clip(1.0 + 0.1 * jax.random.normal(key_list[6], (D,), jnp.float32), 0.5, 1.5).astype(jnp.bfloat16)
    router_weight = noise(key_list[7], (D, EXPERTS), (4 * D) ** -0.5, 0.09375, ((0, 8),))
    expert_in = noise(key_list[8], (D, EXPERTS, 2 * FF), D ** -0.5, 0.1875, ((0, 8),))
    expert_down = noise(key_list[9], (D, EXPERTS, FF), (FF // 16) ** -0.5, 1.0, ((0, 8),))
    cotangent = noise(key_list[10], (SEQS, SEQLEN, D), 1.0, 6.0, ((0, 8), (1, 16)))
    return {"tokens": tokens, "block_order": block_order, "routes": routes, "attn_gain": attn_gain, "qkv_weight": qkv_weight, "proj_weight": proj_weight, "moe_gain": moe_gain, "router_weight": router_weight, "expert_in": expert_in, "expert_down": expert_down, "cotangent": cotangent}


EPSILON = 1e-06
THETA = 10000.0
NEGATIVE = -1e+30
HIGHEST = lax.Precision.HIGHEST

@jax.custom_vjp
def low(v):
    return lax.optimization_barrier(v.astype(jnp.bfloat16)).astype(jnp.float32)

@jax.custom_vjp
def low_back(v):
    return v

def low_keep(v):
    return (low(v), None)

def low_pass(kept, grad):
    return (grad,)

def back_keep(v):
    return (v, None)

def back_low(kept, grad):
    return (low(grad),)
low.defvjp(low_keep, low_pass)
low_back.defvjp(back_keep, back_low)

def rms_scale(values):
    return lax.rsqrt(lax.optimization_barrier(jnp.mean(values * values, axis=-1, keepdims=True)) + EPSILON)

def slot_positions(orders, per_device, blocks):
    within = jnp.arange(per_device, dtype=jnp.int32)
    halfway = per_device // 2
    first = within < halfway
    placed = jnp.where(first[None, :], orders[:, None], blocks - 1 - orders[:, None])
    return (placed * halfway + within[None, :] % halfway).astype(jnp.int32)

def rotary_tables(positions, head_size):
    halfway = head_size // 2
    frequency = THETA ** (-(jnp.arange(halfway, dtype=jnp.float32) * 2.0) / head_size)
    angles = positions.astype(jnp.float32)[:, None] * frequency[None, :]
    return (jnp.cos(angles)[:, None, :], jnp.sin(angles)[:, None, :])

def rotate(values, cos_table, sin_table):
    halfway = values.shape[-1] // 2
    first_half = values[..., :halfway]
    second_half = values[..., halfway:]
    return jnp.concatenate([first_half * cos_table - second_half * sin_table, second_half * cos_table + first_half * sin_table], axis=-1)

def softmax_last(values):
    largest = lax.optimization_barrier(jnp.max(values, axis=-1, keepdims=True))
    exponent = jnp.exp(values - largest)
    return exponent / lax.optimization_barrier(jnp.sum(exponent, axis=-1, keepdims=True))

def expert_block(normed_two, logits, route_rows, expert_in, expert_down):
    expert_ids = jnp.arange(EXPERTS, dtype=jnp.int32)
    picked = route_rows[:, :, None] == expert_ids[None, None, :]
    chosen = lax.optimization_barrier(jnp.sum(picked.astype(jnp.int32), axis=1)).astype(jnp.int32)
    earlier = (jnp.cumsum(chosen, axis=0) - chosen).astype(jnp.int32)
    slot_ids = jnp.arange(CAPACITY, dtype=jnp.int32)
    dispatch = ((chosen.T[:, None, :] == 1) & (earlier.T[:, None, :] == slot_ids[None, :, None])).astype(jnp.float32)
    slot_rows = jnp.einsum('ect,td->ecd', dispatch, normed_two, precision=HIGHEST)
    gate_up = low_back(jnp.einsum('ecd,def->ecf', slot_rows, expert_in, precision=HIGHEST))
    gate_pre = gate_up[..., :FF]
    up_pre = gate_up[..., FF:]
    act = low(gate_pre * jax.nn.sigmoid(gate_pre) * up_pre)
    expert_rows = low(low_back(jnp.einsum('ecf,def->ecd', act, expert_down, precision=HIGHEST)))
    slot_index = lax.optimization_barrier(jnp.sum(jnp.where(picked, earlier[:, None, :], 0), axis=2)).astype(jnp.int32)
    flat_index = (route_rows * CAPACITY + slot_index).astype(jnp.int32)
    token_rows = expert_rows.reshape(EXPERTS * CAPACITY, -1)[flat_index]
    chosen_logits = lax.optimization_barrier(jnp.sum(jnp.where(picked, logits[:, None, :], 0.0), axis=2))
    gate_weights = softmax_last(chosen_logits)
    return jnp.einsum('tk,tkd->td', gate_weights, token_rows, precision=HIGHEST)

def sequence_forward(params, residual_stream, route_rows, block_order):
    attn_gain, qkv_weight, proj_weight, moe_gain, router_weight, expert_in, expert_down = params
    query_width = HEADS * HEAD_DIM
    kv_width = KV_HEADS * HEAD_DIM
    group_size = HEADS // KV_HEADS
    positions = slot_positions(block_order, TOK_DEV, 2 * N_CTX).reshape(SEQLEN)
    cos_table, sin_table = rotary_tables(positions, HEAD_DIM)
    normed_one = low(residual_stream * rms_scale(residual_stream) * attn_gain)
    projected = low_back(jnp.dot(normed_one, qkv_weight, precision=HIGHEST))
    queries = low(rotate(projected[:, :query_width].reshape(SEQLEN, HEADS, HEAD_DIM), cos_table, sin_table))
    keys = low(rotate(projected[:, query_width:query_width + kv_width].reshape(SEQLEN, KV_HEADS, HEAD_DIM), cos_table, sin_table))
    values = low(projected[:, query_width + kv_width:]).reshape(SEQLEN, KV_HEADS, HEAD_DIM)
    block_rows = math.gcd(512, SEQLEN)
    query_blocks = queries.reshape(SEQLEN // block_rows, block_rows, KV_HEADS, group_size, HEAD_DIM)
    position_blocks = positions.reshape(SEQLEN // block_rows, block_rows)
    score_scale = 1.0 / math.sqrt(HEAD_DIM)

    def attend(element):
        query_tile, tile_pos = element
        scores = low_back(jnp.einsum('rgid,sgd->girs', query_tile, keys, precision=HIGHEST) * score_scale)
        visible = positions[None, None, None, :] <= tile_pos[None, None, :, None]
        probs = softmax_last(jnp.where(visible, scores, NEGATIVE))
        return jnp.einsum('girs,sgd->rgid', low(probs), values, precision=HIGHEST)
    attended = lax.map(jax.checkpoint(attend), (query_blocks, position_blocks)).reshape(SEQLEN, query_width)
    attended = low_back(low(attended))
    hidden_state = residual_stream + low_back(jnp.dot(attended, proj_weight.T, precision=HIGHEST))
    normed_two = low(hidden_state * rms_scale(hidden_state) * moe_gain)
    logits = low_back(jnp.dot(normed_two, router_weight, precision=HIGHEST))
    blocked = jax.vmap(expert_block, in_axes=(0, 0, 0, None, None))
    mixture = blocked(normed_two.reshape(N_CTX, TOK_DEV, D), logits.reshape(N_CTX, TOK_DEV, EXPERTS), route_rows.reshape(N_CTX, TOK_DEV, TOPK), expert_in, expert_down)
    return hidden_state + mixture.reshape(SEQLEN, D)

def whole_layer(params, inputs, routes, block_order):

    def one_sequence(residual_stream, route_rows):
        return sequence_forward(params, residual_stream, route_rows, block_order)
    checked = jax.checkpoint(one_sequence)

    def scan_step(carried, element):
        return (carried, checked(element[0], element[1]))
    _, outputs = lax.scan(scan_step, jnp.zeros((), jnp.float32), (inputs, routes))
    return outputs

def reference(tokens, block_order, routes, attn_gain, qkv_weight, proj_weight, moe_gain, router_weight, expert_in, expert_down, cotangent):
    params = (attn_gain.astype(jnp.float32), qkv_weight.astype(jnp.float32), proj_weight.astype(jnp.float32), moe_gain.astype(jnp.float32), router_weight.astype(jnp.float32), expert_in.astype(jnp.float32), expert_down.astype(jnp.float32))
    inputs = tokens.astype(jnp.float32)

    def forward_only(params_in, inputs_in):
        return whole_layer(params_in, inputs_in, routes, block_order)
    outputs, pullback = jax.vjp(forward_only, params, inputs)
    gradients, tokens_grad = pullback(cotangent.astype(jnp.float32))
    return (outputs.astype(jnp.bfloat16), tokens_grad, gradients[0], gradients[1], gradients[2], gradients[3], gradients[4], gradients[5], gradients[6])
```

```python
import math

import jax
import jax.numpy as jnp
from jax import lax
from jax.experimental import pallas as pl
from jax.experimental.pallas import tpu as pltpu
from jax.sharding import PartitionSpec as P

HEAD_DIM = 64
EPSILON = 1e-06
THETA = 10000.0
NEGATIVE = -1e30
BF16 = jnp.bfloat16
F32 = jnp.float32
VMEM_LIMIT = 48 * 1024 * 1024

GROUPS = [[2 * i + c for i in range(8)] for c in range(2)]
PAIRS = [(i, i ^ 1) for i in range(16)]
X_HI = [(i, i ^ 2) for i in range(16)]
X_LO = [(i, i ^ 4) for i in range(8)]
ALONG_Y = [[4 * y + i for y in range(4)] for i in range(4)]
ALONG_Z = [[4 * x + z for z in range(4)] for x in range(2)]


def exchange_ctx(parts):
    return lax.all_to_all(parts, "ctx", 0, 0, tiled=True, axis_index_groups=GROUPS)


def exchange_fsdp(parts):
    return lax.all_to_all(parts, "fsdp", 0, 0, tiled=True)


def copies(own):
    return jnp.broadcast_to(own[None], (8,) + own.shape)


def gather_ctx(own):
    return exchange_ctx(copies(own))


def gather_fsdp(own):
    return exchange_fsdp(copies(own))


def swap_core(own):
    return lax.ppermute(own, "ctx", PAIRS)


def total(parts):
    return jnp.sum(parts.astype(F32), axis=0)


def dot(left, right):
    return jnp.dot(left, right, preferred_element_type=F32)


def dot_tn(left, right):
    return lax.dot_general(left, right, (((0,), (0,)), ((), ())), preferred_element_type=F32)


def dot_nt(left, right):
    return lax.dot_general(left, right, (((1,), (1,)), ((), ())), preferred_element_type=F32)


def query_block(block, half):
    lo = 64 * half
    return jnp.concatenate([block[0:64, lo : lo + 64], block[64:128, lo : lo + 64]], axis=1)


def masked(scores, keys, position):
    rows = lax.broadcasted_iota(jnp.int32, (512, 128), 0) + (keys - 512)
    lanes = lax.broadcasted_iota(jnp.int32, (512, 128), 1) % 64 + position * 64
    tail = jnp.where(rows <= lanes, scores[keys - 512 :], NEGATIVE)
    if keys == 512:
        return tail
    return jnp.concatenate([scores[: keys - 512], tail], axis=0)


def attend_kernel(order_ref, query_ref, own_ref, other_ref, out_ref, rows_ref, cols_ref):
    for number, source_ref in enumerate((own_ref, other_ref)):
        source = source_ref[...].astype(F32).T.astype(BF16)
        for k in range(8):
            b = order_ref[number, k]
            low = pl.multiple_of(b * 64, 64)
            high = pl.multiple_of((31 - b) * 64, 64)
            rows_ref[pl.ds(low, 64), :] = source[128 * k : 128 * k + 64]
            rows_ref[pl.ds(high, 64), :] = source[128 * k + 64 : 128 * k + 128]
    cols_ref[...] = rows_ref[...].astype(F32).T.astype(BF16)
    blank = jnp.zeros((64, 128), BF16)

    def attend(block, half, position, keys):
        right = jnp.concatenate([query_block(block, half), blank], axis=0)
        scores = masked(dot(rows_ref[0:keys, :], right), keys, position)
        exponent = jnp.exp(scores - jnp.max(scores, axis=0, keepdims=True))
        share = 1.0 / jnp.sum(exponent, axis=0, keepdims=True)
        out = dot(cols_ref[64:128, 0:keys], exponent.astype(BF16)) * share
        out = out.T
        return jnp.concatenate([out[0:64], out[64:128]], axis=1).astype(BF16)

    def step(k, carry):
        start = pl.multiple_of(k * 128, 128)
        block = query_ref[:, pl.ds(start, 128)]
        b = order_ref[0, k]

        def both(low_keys, high_keys):
            out_ref[pl.ds(start, 64), :] = attend(block, 0, b, low_keys)
            out_ref[pl.ds(pl.multiple_of(start + 64, 64), 64), :] = attend(
                block, 1, 31 - b, high_keys
            )

        @pl.when(b < 8)
        def _():
            both(512, 2048)

        @pl.when(b >= 8)
        def _():
            both(1024, 1536)

        return carry

    lax.fori_loop(0, 8, step, 0)


def attend_forward(order, query, own, other):
    vmem = pl.BlockSpec(memory_space=pltpu.VMEM)
    return pl.pallas_call(
        attend_kernel,
        out_shape=(
            jax.ShapeDtypeStruct((1024, 128), BF16),
            jax.ShapeDtypeStruct((2048, 128), BF16),
            jax.ShapeDtypeStruct((128, 2048), BF16),
        ),
        in_specs=[pl.BlockSpec(memory_space=pltpu.SMEM), vmem, vmem, vmem],
        out_specs=(vmem, vmem, vmem),
        compiler_params=pltpu.CompilerParams(vmem_limit_bytes=VMEM_LIMIT),
        name="attend_forward",
        cost_estimate=cost(11),
    )(order, query, own, other)


def attend_back_kernel(
    order_ref, query_ref, rows_ref, cols_ref, branch_ref, proj_ref,
    dquery_ref, own_ref, other_ref, acc_ref, grad_ref,
):
    grad_ref[...] = dot(branch_ref[...], proj_ref[...]).astype(BF16)
    acc_ref[...] = jnp.zeros_like(acc_ref)
    blank = jnp.zeros((64, 128), BF16)
    blank_t = jnp.zeros((128, 64), BF16)

    def back(block, grads, half, position, keys):
        query = query_block(block, half)
        query_t = query.astype(F32).T.astype(BF16)
        rows = grads[64 * half : 64 * half + 64]
        grad_t = jnp.concatenate([rows[:, 0:64], rows[:, 64:128]], axis=0)
        grad = grad_t.astype(F32).T.astype(BF16)
        right = jnp.concatenate(
            [jnp.concatenate([query, blank], axis=1), jnp.concatenate([blank, grad], axis=1)],
            axis=0,
        )
        both = dot(rows_ref[0:keys, :], right)
        scores = masked(both[:, 0:128], keys, position)
        dprobs = both[:, 128:256]
        exponent = jnp.exp(scores - jnp.max(scores, axis=0, keepdims=True))
        probs = exponent * (1.0 / jnp.sum(exponent, axis=0, keepdims=True))
        weighted = probs * dprobs
        mean = jnp.sum(weighted, axis=0, keepdims=True)
        dscores = (weighted - probs * mean).astype(BF16)
        pair = jnp.concatenate([dscores, probs.astype(BF16)], axis=1)
        right_t = jnp.concatenate(
            [
                jnp.concatenate([query_t, blank_t], axis=1),
                jnp.concatenate([blank_t, grad_t], axis=1),
            ],
            axis=0,
        )
        acc_ref[0:keys, :] += dot(pair, right_t)
        return dot(cols_ref[0:64, 0:keys], dscores)

    def step(k, carry):
        start = pl.multiple_of(k * 128, 128)
        block = query_ref[:, pl.ds(start, 128)]
        grads = grad_ref[pl.ds(start, 128), :]
        b = order_ref[0, k]

        def both(low_keys, high_keys):
            low = back(block, grads, 0, b, low_keys)
            high = back(block, grads, 1, 31 - b, high_keys)
            dquery_ref[0:64, pl.ds(start, 128)] = jnp.concatenate(
                [low[:, 0:64], high[:, 0:64]], axis=1
            )
            dquery_ref[64:128, pl.ds(start, 128)] = jnp.concatenate(
                [low[:, 64:128], high[:, 64:128]], axis=1
            )

        @pl.when(b < 8)
        def _():
            both(512, 2048)

        @pl.when(b >= 8)
        def _():
            both(1024, 1536)

        return carry

    lax.fori_loop(0, 8, step, 0)
    for number, target_ref in enumerate((own_ref, other_ref)):
        for k in range(8):
            b = order_ref[number, k]
            low = acc_ref[pl.ds(pl.multiple_of(b * 64, 64), 64), :]
            high = acc_ref[pl.ds(pl.multiple_of((31 - b) * 64, 64), 64), :]
            block = jnp.concatenate([low, high], axis=0).T
            target_ref[:, 128 * k : 128 * k + 128] = block.astype(target_ref.dtype)


def attend_backward(order, query, rows, cols, branch, proj):
    vmem = pl.BlockSpec(memory_space=pltpu.VMEM)
    return pl.pallas_call(
        attend_back_kernel,
        out_shape=(
            jax.ShapeDtypeStruct((128, 1024), F32),
            jax.ShapeDtypeStruct((128, 1024), F32),
            jax.ShapeDtypeStruct((128, 1024), BF16),
        ),
        in_specs=[pl.BlockSpec(memory_space=pltpu.SMEM)] + [vmem] * 5,
        out_specs=(vmem, vmem, vmem),
        scratch_shapes=[pltpu.VMEM((2048, 128), F32), pltpu.VMEM((1024, 128), BF16)],
        compiler_params=pltpu.CompilerParams(vmem_limit_bytes=VMEM_LIMIT),
        name="attend_backward",
        cost_estimate=cost(21),
    )(order, query, rows, cols, branch, proj)


def rotate(first, second, cos_table, sin_table):
    return first * cos_table - second * sin_table, second * cos_table + first * sin_table


def cost(microseconds):
    return pl.CostEstimate(
        flops=int(microseconds * 1.1e9), bytes_accessed=int(microseconds * 3e6), transcendentals=0
    )


def vmem_spec():
    return pl.BlockSpec(memory_space=pltpu.VMEM)


def project_kernel(x_ref, weight_ref, cos_ref, sin_ref, normal_ref, query_ref, kv_ref):
    x = x_ref[...].astype(F32)
    rstd = lax.rsqrt(jnp.mean(x * x, axis=-1, keepdims=True) + EPSILON)
    normal = (x * rstd).astype(BF16)
    normal_ref[...] = normal
    mixed = dot(normal, weight_ref[...]).T
    cos_table = cos_ref[...]
    sin_table = sin_ref[...]
    scale = 1.0 / math.sqrt(HEAD_DIM)
    for h in range(3):
        low, high = rotate(
            mixed[64 * h : 64 * h + 32], mixed[64 * h + 32 : 64 * h + 64], cos_table, sin_table
        )
        turned = jnp.concatenate([low, high], axis=0).astype(BF16)
        if h < 2:
            query_ref[64 * h : 64 * h + 64] = (turned.astype(F32) * scale).astype(BF16)
        else:
            kv_ref[0:64] = turned
    kv_ref[64:128] = mixed[192:256].astype(BF16)


def project(x_all, weight, cos_table, sin_table):
    rows = pl.BlockSpec((256, 1024), lambda i: (i, 0))
    columns = pl.BlockSpec((128, 256), lambda i: (0, i))
    table = pl.BlockSpec((32, 256), lambda i: (0, i))
    return pl.pallas_call(
        project_kernel,
        grid=(4,),
        out_shape=(
            jax.ShapeDtypeStruct((1024, 1024), BF16),
            jax.ShapeDtypeStruct((128, 1024), BF16),
            jax.ShapeDtypeStruct((128, 1024), BF16),
        ),
        in_specs=[rows, pl.BlockSpec((1024, 256), lambda i: (0, 0)), table, table],
        out_specs=(rows, columns, columns),
        compiler_params=pltpu.CompilerParams(vmem_limit_bytes=VMEM_LIMIT),
        name="project",
        cost_estimate=cost(2),
    )(x_all, weight, cos_table, sin_table)


def experts_kernel(
    first_ref,
    x_ref,
    attended_ref,
    moe_ref,
    upstream_ref,
    hidden_ref,
    gates_ref,
    normal_ref,
    act_ref,
    dgate_up_ref,
    packed_ref,
):
    first = first_ref[0]
    attended = jnp.concatenate([attended_ref[j] for j in range(8)], axis=1)
    hidden = x_ref[...].astype(F32) + dot_nt(attended, moe_ref[:, 2048:3072])
    hidden_ref[...] = hidden
    rstd = lax.rsqrt(jnp.mean(hidden * hidden, axis=-1, keepdims=True) + EPSILON)
    normal = (hidden * rstd).astype(BF16)
    normal_ref[...] = normal
    lanes = lax.broadcasted_iota(jnp.int32, (256, 128), 1)
    named = upstream_ref[:, 1024:1152].astype(F32).astype(jnp.int32)
    chosen = lanes == named[:, 0:1]
    for k in range(1, 8):
        chosen = chosen | (lanes == named[:, k : k + 1])
    logits = dot(normal, moe_ref[:, 1280:1408])
    held = jnp.where(chosen, logits, NEGATIVE)
    raised = jnp.where(chosen, jnp.exp(held - jnp.max(held, axis=-1, keepdims=True)), 0.0)
    gates = raised / jnp.sum(raised, axis=-1, keepdims=True)
    gates_ref[...] = jnp.where(lanes == 64, rstd, gates)
    gate_up = dot(normal, moe_ref[:, 0:1280])
    spread = dot(upstream_ref[:, 0:1024], moe_ref[:, 1408:2048])
    dgates = jnp.zeros((256, 128), F32)
    dgate_all = []
    dup_all = []
    for c in range(5):
        gate_pre = gate_up[:, 128 * c : 128 * c + 128]
        up_pre = gate_up[:, 640 + 128 * c : 768 + 128 * c]
        back = spread[:, 128 * c : 128 * c + 128]
        weight = jnp.sum(jnp.where(lanes == first + c, gates, 0.0), axis=-1, keepdims=True)
        sigmoid = 1.0 / (1.0 + jnp.exp(-gate_pre))
        silu = gate_pre * sigmoid
        act = silu * up_pre
        act_ref[:, 128 * c : 128 * c + 128] = (weight * act).astype(BF16)
        dact = weight * back
        dgate_all.append(
            (dact * up_pre * sigmoid * (1.0 + gate_pre * (1.0 - sigmoid))).astype(BF16)
        )
        dup_all.append((dact * silu).astype(BF16))
        share = jnp.sum(act * back, axis=-1, keepdims=True)
        dgates = dgates + jnp.where((lanes % 64) == first + c, share, 0.0)
    dgate_up = jnp.concatenate(dgate_all + dup_all, axis=1)
    dgate_up_ref[...] = dgate_up
    packed_ref[:, 0:1024] = dot_nt(dgate_up, moe_ref[:, 0:1280]).astype(BF16)
    high = dgates.astype(BF16)
    low = (dgates - high.astype(F32)).astype(BF16)
    packed_ref[:, 1024:1152] = jnp.where(lanes < 64, high, low)


def experts(first, x_all, attended, moe, upstream):
    def rows(width):
        return pl.BlockSpec((256, width), lambda i: (i, 0))

    return pl.pallas_call(
        experts_kernel,
        grid=(4,),
        out_shape=(
            jax.ShapeDtypeStruct((1024, 1024), F32),
            jax.ShapeDtypeStruct((1024, 128), F32),
            jax.ShapeDtypeStruct((1024, 1024), BF16),
            jax.ShapeDtypeStruct((1024, 640), BF16),
            jax.ShapeDtypeStruct((1024, 1280), BF16),
            jax.ShapeDtypeStruct((1024, 1152), BF16),
        ),
        in_specs=[
            pl.BlockSpec(memory_space=pltpu.SMEM),
            rows(1024),
            pl.BlockSpec((8, 256, 128), lambda i: (0, i, 0)),
            pl.BlockSpec((1024, 3072), lambda i: (0, 0)),
            rows(1152),
        ],
        out_specs=(
            rows(1024),
            rows(128),
            rows(1024),
            rows(640),
            rows(1280),
            rows(1152),
        ),
        compiler_params=pltpu.CompilerParams(vmem_limit_bytes=VMEM_LIMIT),
        name="experts",
        cost_estimate=cost(16),
    )(first, x_all, attended, moe, upstream)


def middle_kernel(
    chip_ref, parts_ref, hidden_ref, gates_ref, upstream_ref, router_ref,
    dhidden_ref, dbranch_ref, dlogits_ref, normal_ref,
):
    summed = parts_ref[0].astype(F32)
    for k in range(1, 8):
        summed = summed + parts_ref[k].astype(F32)
    lanes = lax.broadcasted_iota(jnp.int32, (128, 128), 1)
    gates = jnp.where(lanes < 64, gates_ref[...], 0.0)
    rstd = gates_ref[:, 64:65]
    pair = summed[:, 1024:1152]
    dgates = jnp.where(lanes < 64, pair + pltpu.roll(pair, 64, 1), 0.0)
    dlogits = gates * (dgates - jnp.sum(gates * dgates, axis=-1, keepdims=True))
    dlogits = dlogits.astype(BF16)
    dlogits_ref[...] = dlogits
    scaled = summed[:, 0:1024] + dot_nt(dlogits, router_ref[...])
    normal = hidden_ref[...] * rstd
    normal_ref[...] = normal.astype(BF16)
    dhidden = upstream_ref[...].astype(F32) + rstd * (
        scaled - normal * jnp.mean(scaled * normal, axis=-1, keepdims=True)
    )
    dhidden_ref[...] = dhidden
    dbranch_ref[...] = dhidden.astype(BF16)


def middle(chip, parts, hidden, gates, upstream, moe):
    def own(width):
        return pl.BlockSpec((128, width), lambda i, chip: (chip[0], 0))

    def whole(*shape):
        return pl.BlockSpec(shape, lambda i, chip: (0,) * len(shape))

    return pl.pallas_call(
        middle_kernel,
        grid_spec=pltpu.PrefetchScalarGridSpec(
            num_scalar_prefetch=1,
            grid=(1,),
            in_specs=[
                whole(8, 128, 1152),
                own(1024),
                own(128),
                own(1024),
                pl.BlockSpec((1024, 128), lambda i, chip: (0, 10)),
            ],
            out_specs=(
                whole(128, 1024),
                whole(128, 1024),
                whole(128, 128),
                whole(128, 1024),
            ),
        ),
        out_shape=(
            jax.ShapeDtypeStruct((128, 1024), F32),
            jax.ShapeDtypeStruct((128, 1024), BF16),
            jax.ShapeDtypeStruct((128, 128), BF16),
            jax.ShapeDtypeStruct((128, 1024), BF16),
        ),
        compiler_params=pltpu.CompilerParams(vmem_limit_bytes=VMEM_LIMIT),
        name="middle",
        cost_estimate=cost(2),
    )(chip, parts, hidden, gates, upstream, moe)


def turn_kernel(
    query_ref, own_ref, other_ref, cos_ref, sin_ref, normal_ref, parts_ref, grad_ref
):
    kv = own_ref[...] + other_ref[...].astype(F32)
    cos_table = cos_ref[...]
    sin_table = -sin_ref[...]
    scale = 1.0 / math.sqrt(HEAD_DIM)
    turned = []
    for source in (query_ref[0:64] * scale, query_ref[64:128] * scale, kv[0:64]):
        turned += list(rotate(source[0:32], source[32:64], cos_table, sin_table))
    mixed = jnp.concatenate(turned + [kv[64:128]], axis=0).astype(BF16)
    for k in range(8):
        parts_ref[k] = mixed[:, 128 * k : 128 * k + 128]
    grad_ref[...] = dot(mixed, normal_ref[...]).T.astype(BF16)


def turn(query, own, other, cos_table, sin_table, normal):
    return pl.pallas_call(
        turn_kernel,
        out_shape=(
            jax.ShapeDtypeStruct((8, 256, 128), BF16),
            jax.ShapeDtypeStruct((1024, 256), BF16),
        ),
        in_specs=[vmem_spec()] * 6,
        out_specs=(vmem_spec(), vmem_spec()),
        compiler_params=pltpu.CompilerParams(vmem_limit_bytes=VMEM_LIMIT),
        name="turn",
        cost_estimate=cost(2),
    )(query, own, other, cos_table, sin_table, normal)


def finish_kernel(dmixed_ref, weight_ref, dhidden_ref, x_ref, out_ref):
    dmixed = dmixed_ref[...].astype(F32).T.astype(BF16)
    scaled = dot_nt(dmixed, weight_ref[...])
    x = x_ref[...].astype(F32)
    rstd = lax.rsqrt(jnp.mean(x * x, axis=-1, keepdims=True) + EPSILON)
    normal = x * rstd
    out_ref[...] = dhidden_ref[...] + rstd * (
        scaled - normal * jnp.mean(scaled * normal, axis=-1, keepdims=True)
    )


def finish(dmixed, weight, dhidden, x_own):
    return pl.pallas_call(
        finish_kernel,
        out_shape=jax.ShapeDtypeStruct((128, 1024), F32),
        in_specs=[vmem_spec()] * 4,
        out_specs=vmem_spec(),
        compiler_params=pltpu.CompilerParams(vmem_limit_bytes=VMEM_LIMIT),
        name="finish",
        cost_estimate=cost(2),
    )(dmixed, weight, dhidden, x_own)


def spread_kernel(
    core_ref, own_gate, own_up, own_down, other_gate, other_up, other_down,
    weight_ref, gain_ref, in_ref, down_ref, sums_ref,
):
    @pl.when(pl.program_id(0) == 0)
    def _():
        sums_ref[...] = jnp.zeros_like(sums_ref)

    def write(sources, row):
        gate, up, down = sources
        gain = gain_ref[row : row + 64]
        place = slice(row, row + 64)
        for q in range(4):
            near = 128 * (q + (1 - 2 * (q % 2)) * core_ref[1])
            for source, start in ((gate, 0), (up, 512)):
                lanes = pl.ds(pl.multiple_of(start + near, 128), 128)
                raw = source[q].astype(F32)
                in_ref[0, place, lanes] = raw * gain
                sums_ref[place] += raw * weight_ref[0, place, lanes].astype(F32)
            down_ref[0, place, pl.ds(pl.multiple_of(near, 128), 128)] = down[q].astype(F32)

    own = (own_gate, own_up, own_down)
    other = (other_gate, other_up, other_down)

    @pl.when(core_ref[0] == 0)
    def _():
        write(own, 0)
        write(other, 64)

    @pl.when(core_ref[0] == 1)
    def _():
        write(other, 0)
        write(own, 64)


def spread_experts(core, own, other, weight, gain):
    def piece(start):
        return pl.BlockSpec((4, 64, 128), lambda e: (e // 5, 0, start + e % 5))

    pieces = [piece(0), piece(5), piece(10)]
    return pl.pallas_call(
        spread_kernel,
        grid=(10,),
        out_shape=(
            jax.ShapeDtypeStruct((10, 128, 1024), F32),
            jax.ShapeDtypeStruct((10, 128, 512), F32),
            jax.ShapeDtypeStruct((128, 128), F32),
        ),
        in_specs=[pl.BlockSpec(memory_space=pltpu.SMEM)]
        + pieces
        + pieces
        + [
            pl.BlockSpec((1, 128, 1024), lambda e: (e, 0, 0)),
            pl.BlockSpec((128, 1), lambda e: (0, 0)),
        ],
        out_specs=(
            pl.BlockSpec((1, 128, 1024), lambda e: (e, 0, 0)),
            pl.BlockSpec((1, 128, 512), lambda e: (e, 0, 0)),
            pl.BlockSpec((128, 128), lambda e: (0, 0)),
        ),
        compiler_params=pltpu.CompilerParams(vmem_limit_bytes=VMEM_LIMIT),
        name="spread_experts",
        cost_estimate=cost(9),
    )(core, own, own, own, other, other, other, weight, gain)


def spread_attention_kernel(
    core_ref, own_ref, other_ref, weight_ref, gain_ref, qkv_ref, proj_ref, router_ref, sums_ref
):
    def write(source_ref, row):
        gain = gain_ref[row : row + 64]
        place = slice(row, row + 64)
        raw = [source_ref[j].astype(F32) for j in range(8)]
        query = jnp.concatenate([part[:, 0:128] for part in raw], axis=1)
        key = jnp.concatenate([part[:, 128:192] for part in raw], axis=1)
        value = jnp.concatenate([part[:, 192:256] for part in raw], axis=1)
        qkv = jnp.concatenate([query, key, value], axis=1)
        qkv_ref[place] = qkv * gain
        sums_ref[place] = jnp.sum(qkv * weight_ref[place].astype(F32), axis=-1, keepdims=True)
        router = raw[0][:, 384:512]
        for j in range(8):
            proj_ref[place, 128 * j : 128 * j + 128] = raw[j][:, 256:384]
            if j > 0:
                router = router + raw[j][:, 384:512]
        router_ref[place] = router

    @pl.when(core_ref[0] == 0)
    def _():
        write(own_ref, 0)
        write(other_ref, 64)

    @pl.when(core_ref[0] == 1)
    def _():
        write(other_ref, 0)
        write(own_ref, 64)


def spread_attention(core, own, other, weight, gain):
    return pl.pallas_call(
        spread_attention_kernel,
        out_shape=(
            jax.ShapeDtypeStruct((128, 2048), F32),
            jax.ShapeDtypeStruct((128, 1024), F32),
            jax.ShapeDtypeStruct((128, 128), F32),
            jax.ShapeDtypeStruct((128, 1), F32),
        ),
        in_specs=[pl.BlockSpec(memory_space=pltpu.SMEM)] + [vmem_spec()] * 4,
        out_specs=tuple([vmem_spec()] * 4),
        compiler_params=pltpu.CompilerParams(vmem_limit_bytes=VMEM_LIMIT),
        name="spread_attention",
        cost_estimate=cost(2),
    )(core, own, other, weight, gain)


def fold_cores(core, parts):
    split = parts.reshape(8, 2, 64, parts.shape[2])
    mine = jnp.where(core == 0, split[:, 0], split[:, 1])
    theirs = jnp.where(core == 0, split[:, 1], split[:, 0])
    return (mine.astype(F32) + swap_core(theirs).astype(F32)).astype(BF16)


def gather_weights(pair):
    return lax.all_gather(pair, "fsdp", axis=0, tiled=False, axis_index_groups=ALONG_Z)


def join_weights(core, x_lo, gathered):
    other = swap_core(gathered)
    low = jnp.where(core == 0, gathered, other)
    high = jnp.where(core == 0, other, gathered)
    joined = jnp.stack([low, high], axis=2)
    first = jnp.where(x_lo == 0, joined[:, 0], joined[:, 1])
    second = jnp.where(x_lo == 0, joined[:, 1], joined[:, 0])
    return jnp.stack([first, second]).reshape(1024, gathered.shape[3])


def scatter_experts(x_lo, parts):
    split = parts.reshape(2, 4, 64, parts.shape[2])
    mine = jnp.where(x_lo == 0, split[0], split[1])
    theirs = jnp.where(x_lo == 0, split[1], split[0])
    return lax.psum_scatter(
        jnp.stack([mine, theirs], axis=1).reshape(512, parts.shape[2]),
        "fsdp",
        scatter_dimension=0,
        tiled=True,
        axis_index_groups=ALONG_Z,
    )


def body(
    tokens,
    block_order,
    routes,
    attn_gain,
    qkv_weight,
    proj_weight,
    moe_gain,
    router_weight,
    expert_in,
    expert_down,
    cotangent,
):
    index = lax.axis_index("ctx")
    chip = index // 2
    core = index % 2
    x_hi = chip % 2
    x_lo = lax.axis_index("fsdp") // 4
    x_own = tokens.reshape(128, 1024)
    g_own = cotangent.reshape(128, 1024)
    gain_one = attn_gain.astype(F32)[:, None]
    gain_two = moe_gain.astype(F32)[:, None]

    qkv_turned = jnp.concatenate(
        [
            qkv_weight[:, 0:1024].reshape(128, 8, 128),
            qkv_weight[:, 1024:1536].reshape(128, 8, 64),
            qkv_weight[:, 1536:2048].reshape(128, 8, 64),
        ],
        axis=2,
    ).reshape(128, 2048)
    qkv_turned = (qkv_turned.astype(F32) * gain_one).astype(BF16)
    qkv_part = lax.dynamic_slice(qkv_turned, (0, 256 * chip), (128, 256))
    qkv_slice = gather_fsdp(qkv_part).reshape(1024, 256)

    proj_half = lax.dynamic_slice(proj_weight, (64 * core, 0), (64, 1024))
    first = 5 * (chip // 4)
    lane = 128 * (chip % 4)
    in_by_expert = expert_in.transpose(1, 0, 2)
    down_by_expert = expert_down.transpose(1, 0, 2)
    row = 64 * core

    def piece(source, offset):
        taken = lax.dynamic_slice(source, (first, row, offset + lane), (5, 64, 128))
        return taken.transpose(1, 0, 2).reshape(64, 640)

    router_half = lax.dynamic_slice(router_weight, (row, 0), (64, 10))
    gain_half = lax.dynamic_slice(gain_two, (row, 0), (64, 1))
    with_gain = jnp.concatenate(
        [piece(in_by_expert, 0), piece(in_by_expert, 512)]
        + [jnp.pad(router_half, ((0, 0), (0, 118)))],
        axis=1,
    )
    with_gain = (with_gain.astype(F32) * gain_half).astype(BF16)
    moe_half = jnp.concatenate([with_gain, piece(down_by_expert, 0), proj_half], axis=1)
    moe_other = lax.ppermute(moe_half, "fsdp", X_LO)
    qkv_half = lax.dynamic_slice(qkv_turned, (row, 0), (64, 2048))
    qkv_other = lax.ppermute(qkv_half, "fsdp", X_LO)
    qkv_slice, moe_pieces, x_copies = lax.optimization_barrier(
        (qkv_slice, jnp.stack([moe_half, moe_other]), copies(x_own))
    )
    moe_gathered = gather_weights(moe_pieces)
    x_all = exchange_ctx(x_copies).reshape(1024, 1024)

    routes_low = jnp.pad(routes.reshape(128, 8).astype(BF16), ((0, 0), (0, 120)))
    g_copies = copies(jnp.concatenate([g_own, routes_low], axis=1))
    x_all, g_copies = lax.optimization_barrier((x_all, g_copies))
    upstream = exchange_ctx(g_copies).reshape(1024, 1152)

    orders = block_order.reshape(8, 2)
    order_own = jnp.where(core == 0, orders[:, 0], orders[:, 1])
    order_other = jnp.where(core == 0, orders[:, 1], orders[:, 0])
    order = jnp.stack([order_own, order_other])
    within = jnp.arange(128, dtype=jnp.int32)
    placed = jnp.where(within[None, :] < 64, order_own[:, None], 31 - order_own[:, None])
    positions = (placed * 64 + within[None, :] % 64).reshape(1, 1024)
    frequency = THETA ** (-(jnp.arange(32, dtype=F32) * 2.0) / HEAD_DIM)
    angles = frequency[:, None] * positions.astype(F32)
    cos_table = jnp.cos(angles)
    sin_table = jnp.sin(angles)

    xh_one, query, key_value = project(
        x_all,
        qkv_slice,
        cos_table,
        sin_table,
    )
    attended, kv_rows, kv_cols = attend_forward(order, query, key_value, swap_core(key_value))

    attended, upstream, moe_gathered, qkv_pieces = lax.optimization_barrier(
        (attended, upstream, moe_gathered, jnp.stack([qkv_half, qkv_other]))
    )
    moe_full = join_weights(core, x_lo, moe_gathered)
    qkv_gathered = gather_weights(qkv_pieces)

    hidden, gates, xh_two, act_gated, dgate_up, packed = experts(
        first.reshape(1).astype(jnp.int32),
        x_all,
        gather_ctx(attended),
        moe_full,
        upstream,
    )
    packed, qkv_gathered = lax.optimization_barrier((packed, qkv_gathered))
    parts = exchange_ctx(packed.reshape(8, 128, 1152))

    down_slice = moe_full[:, 1408:2048]
    out_part = dot_nt(act_gated, down_slice).astype(BF16)
    in_grad = dot_tn(xh_two, dgate_up).astype(BF16)
    down_grad = dot_tn(upstream[:, 0:1024], act_gated).astype(BF16)
    moe_fold = fold_cores(
        core, jnp.concatenate([in_grad, down_grad], axis=1).reshape(8, 128, 1920)
    )
    proj_slice = lax.dynamic_slice(moe_full, (0, 2048 + 128 * chip), (1024, 128))
    parts, out_part, moe_fold, proj_slice = lax.optimization_barrier(
        (parts, out_part, moe_fold, proj_slice)
    )
    moe_sum = scatter_experts(x_lo, moe_fold).reshape(2, 64, 1920)
    moe_near = lax.ppermute(moe_sum[1], "fsdp", X_LO)

    own_rows = 128 * chip
    hidden_own = lax.dynamic_slice(hidden, (own_rows, 0), (128, 1024))
    dhidden, dbranch, dlogits, normal_two = middle(
        chip.reshape(1).astype(jnp.int32), parts, hidden, gates, upstream, moe_full
    )
    dbranch_all = gather_ctx(dbranch).reshape(1024, 1024)
    qkv_full = join_weights(core, x_lo, qkv_gathered)
    dbranch_all, out_part, qkv_full, moe_near = lax.optimization_barrier(
        (dbranch_all, out_part, qkv_full, moe_near)
    )
    moe_sum = (moe_sum[0].astype(F32) + moe_near.astype(F32)).astype(BF16)
    moe_pair = jnp.stack([moe_sum, lax.ppermute(moe_sum, "ctx", X_HI)])
    out_parts = exchange_ctx(out_part.reshape(8, 128, 1024))
    router_part = dot_tn(normal_two, dlogits).astype(BF16)
    proj_part = dot_tn(dbranch_all, attended).astype(BF16)

    dquery, dkv_own, dkv_other = attend_backward(
        order, query, kv_rows, kv_cols, dbranch_all, proj_slice
    )
    dkv_other, out_parts, moe_pair = lax.optimization_barrier((dkv_other, out_parts, moe_pair))
    moe_own = lax.all_gather(moe_pair, "ctx", axis=0, tiled=True, axis_index_groups=ALONG_Y)
    layer_out = (hidden_own + total(out_parts)).astype(BF16)
    dmixed, qkv_part_grad = turn(
        dquery, dkv_own, swap_core(dkv_other), cos_table, sin_table, xh_one
    )
    attn_fold = fold_cores(
        core,
        jnp.concatenate([qkv_part_grad, proj_part, router_part], axis=1).reshape(8, 128, 512),
    )
    attn_parts, moe_own = lax.optimization_barrier((exchange_fsdp(attn_fold), moe_own))
    attn_sum = total(attn_parts).astype(BF16).reshape(1, 256, 128)
    tail = exchange_ctx(
        jnp.concatenate([dmixed, jnp.broadcast_to(attn_sum, (8, 256, 128))], axis=1)
    )
    in_grad, down_grad, gain_sums = spread_experts(
        jnp.stack([core, x_hi]).astype(jnp.int32),
        moe_own,
        swap_core(moe_own),
        in_by_expert,
        gain_two,
    )
    tail, in_grad, down_grad, gain_sums = lax.optimization_barrier(
        (tail, in_grad, down_grad, gain_sums)
    )
    dmixed_own = tail[:, 0:256].reshape(2048, 128)
    attn_own = tail[:, 256:512].reshape(8, 64, 512)
    tokens_grad = finish(dmixed_own, qkv_full, dhidden, x_own)
    qkv_grad, proj_grad, router_raw, attn_gain_grad = spread_attention(
        core.reshape(1).astype(jnp.int32), attn_own, swap_core(attn_own), qkv_weight, gain_one
    )
    router_raw = router_raw[:, 0:10]
    attn_gain_grad = attn_gain_grad.reshape(128)
    expert_in_grad = in_grad.transpose(1, 0, 2)
    expert_down_grad = down_grad.transpose(1, 0, 2)
    router_grad = router_raw * gain_two
    moe_gain_grad = jnp.sum(gain_sums, axis=1) + jnp.sum(
        router_raw * router_weight.astype(F32), axis=1
    )
    return (
        layer_out.reshape(1, 128, 1024),
        tokens_grad.reshape(1, 128, 1024),
        attn_gain_grad,
        qkv_grad,
        proj_grad,
        moe_gain_grad,
        router_grad,
        expert_in_grad,
        expert_down_grad,
    )


def solution(mesh):
    in_specs = (
        P("fsdp", "ctx", None),
        P(),
        P("fsdp", "ctx", None),
        P("fsdp"),
        P("fsdp", None),
        P("fsdp", None),
        P("fsdp"),
        P("fsdp", None),
        P("fsdp", None, None),
        P("fsdp", None, None),
        P("fsdp", "ctx", None),
    )
    out_specs = (
        P("fsdp", "ctx", None),
        P("fsdp", "ctx", None),
        P("fsdp"),
        P("fsdp", None),
        P("fsdp", None),
        P("fsdp"),
        P("fsdp", None),
        P("fsdp", None, None),
        P("fsdp", None, None),
    )
    return jax.shard_map(body, mesh=mesh, in_specs=in_specs, out_specs=out_specs, check_vma=False)
```

```python
import math

import jax
import jax.numpy as jnp
from jax import lax
from jax.experimental import pallas as pl
from jax.experimental.pallas import tpu as pltpu
from jax.sharding import PartitionSpec as P

HEAD_DIM = 64
EPSILON = 1e-06
THETA = 10000.0
NEGATIVE = -1e30
BF16 = jnp.bfloat16
F32 = jnp.float32
VMEM_LIMIT = 48 * 1024 * 1024

GROUPS = [[2 * i + c for i in range(8)] for c in range(2)]
PAIRS = [(i, i ^ 1) for i in range(16)]
X_HI = [(i, i ^ 2) for i in range(16)]
X_LO = [(i, i ^ 4) for i in range(8)]
ALONG_Y = [[4 * y + i for y in range(4)] for i in range(4)]
ALONG_Z = [[4 * x + z for z in range(4)] for x in range(2)]


def exchange_ctx(parts):
    return lax.all_to_all(parts, "ctx", 0, 0, tiled=True, axis_index_groups=GROUPS)


def exchange_fsdp(parts):
    return lax.all_to_all(parts, "fsdp", 0, 0, tiled=True)


def copies(own):
    return jnp.broadcast_to(own[None], (8,) + own.shape)


def gather_ctx(own):
    return exchange_ctx(copies(own))


def gather_fsdp(own):
    return exchange_fsdp(copies(own))


def swap_core(own):
    return lax.ppermute(own, "ctx", PAIRS)


def total(parts):
    return jnp.sum(parts.astype(F32), axis=0)


def dot(left, right):
    return jnp.dot(left, right, preferred_element_type=F32)


def dot_tn(left, right):
    return lax.dot_general(left, right, (((0,), (0,)), ((), ())), preferred_element_type=F32)


def dot_nt(left, right):
    return lax.dot_general(left, right, (((1,), (1,)), ((), ())), preferred_element_type=F32)


def query_block(block, half):
    lo = 64 * half
    return jnp.concatenate([block[0:64, lo : lo + 64], block[64:128, lo : lo + 64]], axis=1)


def masked(scores, keys, position):
    rows = lax.broadcasted_iota(jnp.int32, (512, 128), 0) + (keys - 512)
    lanes = lax.broadcasted_iota(jnp.int32, (512, 128), 1) % 64 + position * 64
    tail = jnp.where(rows <= lanes, scores[keys - 512 :], NEGATIVE)
    if keys == 512:
        return tail
    return jnp.concatenate([scores[: keys - 512], tail], axis=0)


def attend_kernel(order_ref, query_ref, own_ref, other_ref, out_ref, rows_ref, cols_ref):
    for number, source_ref in enumerate((own_ref, other_ref)):
        source = source_ref[...].astype(F32).T.astype(BF16)
        for k in range(8):
            b = order_ref[number, k]
            low = pl.multiple_of(b * 64, 64)
            high = pl.multiple_of((31 - b) * 64, 64)
            rows_ref[pl.ds(low, 64), :] = source[128 * k : 128 * k + 64]
            rows_ref[pl.ds(high, 64), :] = source[128 * k + 64 : 128 * k + 128]
    cols_ref[...] = rows_ref[...].astype(F32).T.astype(BF16)
    blank = jnp.zeros((64, 128), BF16)

    def attend(block, half, position, keys):
        right = jnp.concatenate([query_block(block, half), blank], axis=0)
        scores = masked(dot(rows_ref[0:keys, :], right), keys, position)
        exponent = jnp.exp(scores - jnp.max(scores, axis=0, keepdims=True))
        share = 1.0 / jnp.sum(exponent, axis=0, keepdims=True)
        out = dot(cols_ref[64:128, 0:keys], exponent.astype(BF16)) * share
        out = out.T
        return jnp.concatenate([out[0:64], out[64:128]], axis=1).astype(BF16)

    def step(k, carry):
        start = pl.multiple_of(k * 128, 128)
        block = query_ref[:, pl.ds(start, 128)]
        b = order_ref[0, k]

        def both(low_keys, high_keys):
            out_ref[pl.ds(start, 64), :] = attend(block, 0, b, low_keys)
            out_ref[pl.ds(pl.multiple_of(start + 64, 64), 64), :] = attend(
                block, 1, 31 - b, high_keys
            )

        @pl.when(b < 8)
        def _():
            both(512, 2048)

        @pl.when(b >= 8)
        def _():
            both(1024, 1536)

        return carry

    lax.fori_loop(0, 8, step, 0)


def attend_forward(order, query, own, other):
    vmem = pl.BlockSpec(memory_space=pltpu.VMEM)
    return pl.pallas_call(
        attend_kernel,
        out_shape=(
            jax.ShapeDtypeStruct((1024, 128), BF16),
            jax.ShapeDtypeStruct((2048, 128), BF16),
            jax.ShapeDtypeStruct((128, 2048), BF16),
        ),
        in_specs=[pl.BlockSpec(memory_space=pltpu.SMEM), vmem, vmem, vmem],
        out_specs=(vmem, vmem, vmem),
        compiler_params=pltpu.CompilerParams(vmem_limit_bytes=VMEM_LIMIT),
        name="attend_forward",
        cost_estimate=cost(11),
    )(order, query, own, other)


def attend_back_kernel(
    order_ref, query_ref, rows_ref, cols_ref, branch_ref, proj_ref,
    dquery_ref, own_ref, other_ref, acc_ref, grad_ref,
):
    grad_ref[...] = dot(branch_ref[...], proj_ref[...]).astype(BF16)
    acc_ref[...] = jnp.zeros_like(acc_ref)
    blank = jnp.zeros((64, 128), BF16)
    blank_t = jnp.zeros((128, 64), BF16)

    def back(block, grads, half, position, keys):
        query = query_block(block, half)
        query_t = query.astype(F32).T.astype(BF16)
        rows = grads[64 * half : 64 * half + 64]
        grad_t = jnp.concatenate([rows[:, 0:64], rows[:, 64:128]], axis=0)
        grad = grad_t.astype(F32).T.astype(BF16)
        right = jnp.concatenate(
            [jnp.concatenate([query, blank], axis=1), jnp.concatenate([blank, grad], axis=1)],
            axis=0,
        )
        both = dot(rows_ref[0:keys, :], right)
        scores = masked(both[:, 0:128], keys, position)
        dprobs = both[:, 128:256]
        exponent = jnp.exp(scores - jnp.max(scores, axis=0, keepdims=True))
        probs = exponent * (1.0 / jnp.sum(exponent, axis=0, keepdims=True))
        weighted = probs * dprobs
        mean = jnp.sum(weighted, axis=0, keepdims=True)
        dscores = (weighted - probs * mean).astype(BF16)
        pair = jnp.concatenate([dscores, probs.astype(BF16)], axis=1)
        right_t = jnp.concatenate(
            [
                jnp.concatenate([query_t, blank_t], axis=1),
                jnp.concatenate([blank_t, grad_t], axis=1),
            ],
            axis=0,
        )
        acc_ref[0:keys, :] += dot(pair, right_t)
        return dot(cols_ref[0:64, 0:keys], dscores)

    def step(k, carry):
        start = pl.multiple_of(k * 128, 128)
        block = query_ref[:, pl.ds(start, 128)]
        grads = grad_ref[pl.ds(start, 128), :]
        b = order_ref[0, k]

        def both(low_keys, high_keys):
            low = back(block, grads, 0, b, low_keys)
            high = back(block, grads, 1, 31 - b, high_keys)
            dquery_ref[0:64, pl.ds(start, 128)] = jnp.concatenate(
                [low[:, 0:64], high[:, 0:64]], axis=1
            )
            dquery_ref[64:128, pl.ds(start, 128)] = jnp.concatenate(
                [low[:, 64:128], high[:, 64:128]], axis=1
            )

        @pl.when(b < 8)
        def _():
            both(512, 2048)

        @pl.when(b >= 8)
        def _():
            both(1024, 1536)

        return carry

    lax.fori_loop(0, 8, step, 0)
    for number, target_ref in enumerate((own_ref, other_ref)):
        for k in range(8):
            b = order_ref[number, k]
            low = acc_ref[pl.ds(pl.multiple_of(b * 64, 64), 64), :]
            high = acc_ref[pl.ds(pl.multiple_of((31 - b) * 64, 64), 64), :]
            block = jnp.concatenate([low, high], axis=0).T
            target_ref[:, 128 * k : 128 * k + 128] = block.astype(target_ref.dtype)


def attend_backward(order, query, rows, cols, branch, proj):
    vmem = pl.BlockSpec(memory_space=pltpu.VMEM)
    return pl.pallas_call(
        attend_back_kernel,
        out_shape=(
            jax.ShapeDtypeStruct((128, 1024), F32),
            jax.ShapeDtypeStruct((128, 1024), F32),
            jax.ShapeDtypeStruct((128, 1024), BF16),
        ),
        in_specs=[pl.BlockSpec(memory_space=pltpu.SMEM)] + [vmem] * 5,
        out_specs=(vmem, vmem, vmem),
        scratch_shapes=[pltpu.VMEM((2048, 128), F32), pltpu.VMEM((1024, 128), BF16)],
        compiler_params=pltpu.CompilerParams(vmem_limit_bytes=VMEM_LIMIT),
        name="attend_backward",
        cost_estimate=cost(21),
    )(order, query, rows, cols, branch, proj)


def rotate(first, second, cos_table, sin_table):
    return first * cos_table - second * sin_table, second * cos_table + first * sin_table


def cost(microseconds):
    return pl.CostEstimate(
        flops=int(microseconds * 1.1e9), bytes_accessed=int(microseconds * 3e6), transcendentals=0
    )


def vmem_spec():
    return pl.BlockSpec(memory_space=pltpu.VMEM)


def project_kernel(x_ref, weight_ref, cos_ref, sin_ref, normal_ref, query_ref, kv_ref):
    x = x_ref[...].astype(F32)
    rstd = lax.rsqrt(jnp.mean(x * x, axis=-1, keepdims=True) + EPSILON)
    normal = (x * rstd).astype(BF16)
    normal_ref[...] = normal
    mixed = dot(normal, weight_ref[...]).T
    cos_table = cos_ref[...]
    sin_table = sin_ref[...]
    scale = 1.0 / math.sqrt(HEAD_DIM)
    for h in range(3):
        low, high = rotate(
            mixed[64 * h : 64 * h + 32], mixed[64 * h + 32 : 64 * h + 64], cos_table, sin_table
        )
        turned = jnp.concatenate([low, high], axis=0).astype(BF16)
        if h < 2:
            query_ref[64 * h : 64 * h + 64] = (turned.astype(F32) * scale).astype(BF16)
        else:
            kv_ref[0:64] = turned
    kv_ref[64:128] = mixed[192:256].astype(BF16)


def project(x_all, weight, cos_table, sin_table):
    rows = pl.BlockSpec((256, 1024), lambda i: (i, 0))
    columns = pl.BlockSpec((128, 256), lambda i: (0, i))
    table = pl.BlockSpec((32, 256), lambda i: (0, i))
    return pl.pallas_call(
        project_kernel,
        grid=(4,),
        out_shape=(
            jax.ShapeDtypeStruct((1024, 1024), BF16),
            jax.ShapeDtypeStruct((128, 1024), BF16),
            jax.ShapeDtypeStruct((128, 1024), BF16),
        ),
        in_specs=[rows, pl.BlockSpec((1024, 256), lambda i: (0, 0)), table, table],
        out_specs=(rows, columns, columns),
        compiler_params=pltpu.CompilerParams(vmem_limit_bytes=VMEM_LIMIT),
        name="project",
        cost_estimate=cost(2),
    )(x_all, weight, cos_table, sin_table)


def experts_kernel(
    first_ref,
    x_ref,
    attended_ref,
    moe_ref,
    upstream_ref,
    hidden_ref,
    gates_ref,
    normal_ref,
    act_ref,
    dgate_up_ref,
    packed_ref,
):
    first = first_ref[0]
    attended = jnp.concatenate([attended_ref[j] for j in range(8)], axis=1)
    hidden = x_ref[...].astype(F32) + dot_nt(attended, moe_ref[:, 2048:3072])
    hidden_ref[...] = hidden
    rstd = lax.rsqrt(jnp.mean(hidden * hidden, axis=-1, keepdims=True) + EPSILON)
    normal = (hidden * rstd).astype(BF16)
    normal_ref[...] = normal
    lanes = lax.broadcasted_iota(jnp.int32, (256, 128), 1)
    named = upstream_ref[:, 1024:1152].astype(F32).astype(jnp.int32)
    chosen = lanes == named[:, 0:1]
    for k in range(1, 8):
        chosen = chosen | (lanes == named[:, k : k + 1])
    logits = dot(normal, moe_ref[:, 1280:1408])
    held = jnp.where(chosen, logits, NEGATIVE)
    raised = jnp.where(chosen, jnp.exp(held - jnp.max(held, axis=-1, keepdims=True)), 0.0)
    gates = raised / jnp.sum(raised, axis=-1, keepdims=True)
    gates_ref[...] = jnp.where(lanes == 64, rstd, gates)
    gate_up = dot(normal, moe_ref[:, 0:1280])
    spread = dot(upstream_ref[:, 0:1024], moe_ref[:, 1408:2048])
    dgates = jnp.zeros((256, 128), F32)
    dgate_all = []
    dup_all = []
    for c in range(5):
        gate_pre = gate_up[:, 128 * c : 128 * c + 128]
        up_pre = gate_up[:, 640 + 128 * c : 768 + 128 * c]
        back = spread[:, 128 * c : 128 * c + 128]
        weight = jnp.sum(jnp.where(lanes == first + c, gates, 0.0), axis=-1, keepdims=True)
        sigmoid = 1.0 / (1.0 + jnp.exp(-gate_pre))
        silu = gate_pre * sigmoid
        act = silu * up_pre
        act_ref[:, 128 * c : 128 * c + 128] = (weight * act).astype(BF16)
        dact = weight * back
        dgate_all.append(
            (dact * up_pre * sigmoid * (1.0 + gate_pre * (1.0 - sigmoid))).astype(BF16)
        )
        dup_all.append((dact * silu).astype(BF16))
        share = jnp.sum(act * back, axis=-1, keepdims=True)
        dgates = dgates + jnp.where((lanes % 64) == first + c, share, 0.0)
    dgate_up = jnp.concatenate(dgate_all + dup_all, axis=1)
    dgate_up_ref[...] = dgate_up
    packed_ref[:, 0:1024] = dot_nt(dgate_up, moe_ref[:, 0:1280]).astype(BF16)
    high = dgates.astype(BF16)
    low = (dgates - high.astype(F32)).astype(BF16)
    packed_ref[:, 1024:1152] = jnp.where(lanes < 64, high, low)


def experts(first, x_all, attended, moe, upstream):
    def rows(width):
        return pl.BlockSpec((256, width), lambda i: (i, 0))

    return pl.pallas_call(
        experts_kernel,
        grid=(4,),
        out_shape=(
            jax.ShapeDtypeStruct((1024, 1024), F32),
            jax.ShapeDtypeStruct((1024, 128), F32),
            jax.ShapeDtypeStruct((1024, 1024), BF16),
            jax.ShapeDtypeStruct((1024, 640), BF16),
            jax.ShapeDtypeStruct((1024, 1280), BF16),
            jax.ShapeDtypeStruct((1024, 1152), BF16),
        ),
        in_specs=[
            pl.BlockSpec(memory_space=pltpu.SMEM),
            rows(1024),
            pl.BlockSpec((8, 256, 128), lambda i: (0, i, 0)),
            pl.BlockSpec((1024, 3072), lambda i: (0, 0)),
            rows(1152),
        ],
        out_specs=(
            rows(1024),
            rows(128),
            rows(1024),
            rows(640),
            rows(1280),
            rows(1152),
        ),
        compiler_params=pltpu.CompilerParams(vmem_limit_bytes=VMEM_LIMIT),
        name="experts",
        cost_estimate=cost(16),
    )(first, x_all, attended, moe, upstream)


def middle_kernel(
    chip_ref, parts_ref, hidden_ref, gates_ref, upstream_ref, router_ref,
    dhidden_ref, dbranch_ref, dlogits_ref, normal_ref,
):
    summed = parts_ref[0].astype(F32)
    for k in range(1, 8):
        summed = summed + parts_ref[k].astype(F32)
    lanes = lax.broadcasted_iota(jnp.int32, (128, 128), 1)
    gates = jnp.where(lanes < 64, gates_ref[...], 0.0)
    rstd = gates_ref[:, 64:65]
    pair = summed[:, 1024:1152]
    dgates = jnp.where(lanes < 64, pair + pltpu.roll(pair, 64, 1), 0.0)
    dlogits = gates * (dgates - jnp.sum(gates * dgates, axis=-1, keepdims=True))
    dlogits = dlogits.astype(BF16)
    dlogits_ref[...] = dlogits
    scaled = summed[:, 0:1024] + dot_nt(dlogits, router_ref[...])
    normal = hidden_ref[...] * rstd
    normal_ref[...] = normal.astype(BF16)
    dhidden = upstream_ref[...].astype(F32) + rstd * (
        scaled - normal * jnp.mean(scaled * normal, axis=-1, keepdims=True)
    )
    dhidden_ref[...] = dhidden
    dbranch_ref[...] = dhidden.astype(BF16)


def middle(chip, parts, hidden, gates, upstream, moe):
    def own(width):
        return pl.BlockSpec((128, width), lambda i, chip: (chip[0], 0))

    def whole(*shape):
        return pl.BlockSpec(shape, lambda i, chip: (0,) * len(shape))

    return pl.pallas_call(
        middle_kernel,
        grid_spec=pltpu.PrefetchScalarGridSpec(
            num_scalar_prefetch=1,
            grid=(1,),
            in_specs=[
                whole(8, 128, 1152),
                own(1024),
                own(128),
                own(1024),
                pl.BlockSpec((1024, 128), lambda i, chip: (0, 10)),
            ],
            out_specs=(
                whole(128, 1024),
                whole(128, 1024),
                whole(128, 128),
                whole(128, 1024),
            ),
        ),
        out_shape=(
            jax.ShapeDtypeStruct((128, 1024), F32),
            jax.ShapeDtypeStruct((128, 1024), BF16),
            jax.ShapeDtypeStruct((128, 128), BF16),
            jax.ShapeDtypeStruct((128, 1024), BF16),
        ),
        compiler_params=pltpu.CompilerParams(vmem_limit_bytes=VMEM_LIMIT),
        name="middle",
        cost_estimate=cost(2),
    )(chip, parts, hidden, gates, upstream, moe)


def turn_kernel(
    query_ref, own_ref, other_ref, cos_ref, sin_ref, normal_ref, parts_ref, grad_ref
):
    kv = own_ref[...] + other_ref[...].astype(F32)
    cos_table = cos_ref[...]
    sin_table = -sin_ref[...]
    scale = 1.0 / math.sqrt(HEAD_DIM)
    turned = []
    for source in (query_ref[0:64] * scale, query_ref[64:128] * scale, kv[0:64]):
        turned += list(rotate(source[0:32], source[32:64], cos_table, sin_table))
    mixed = jnp.concatenate(turned + [kv[64:128]], axis=0).astype(BF16)
    for k in range(8):
        parts_ref[k] = mixed[:, 128 * k : 128 * k + 128]
    grad_ref[...] = dot(mixed, normal_ref[...]).T.astype(BF16)


def turn(query, own, other, cos_table, sin_table, normal):
    return pl.pallas_call(
        turn_kernel,
        out_shape=(
            jax.ShapeDtypeStruct((8, 256, 128), BF16),
            jax.ShapeDtypeStruct((1024, 256), BF16),
        ),
        in_specs=[vmem_spec()] * 6,
        out_specs=(vmem_spec(), vmem_spec()),
        compiler_params=pltpu.CompilerParams(vmem_limit_bytes=VMEM_LIMIT),
        name="turn",
        cost_estimate=cost(2),
    )(query, own, other, cos_table, sin_table, normal)


def finish_kernel(dmixed_ref, weight_ref, dhidden_ref, x_ref, out_ref):
    dmixed = dmixed_ref[...].astype(F32).T.astype(BF16)
    scaled = dot_nt(dmixed, weight_ref[...])
    x = x_ref[...].astype(F32)
    rstd = lax.rsqrt(jnp.mean(x * x, axis=-1, keepdims=True) + EPSILON)
    normal = x * rstd
    out_ref[...] = dhidden_ref[...] + rstd * (
        scaled - normal * jnp.mean(scaled * normal, axis=-1, keepdims=True)
    )


def finish(dmixed, weight, dhidden, x_own):
    return pl.pallas_call(
        finish_kernel,
        out_shape=jax.ShapeDtypeStruct((128, 1024), F32),
        in_specs=[vmem_spec()] * 4,
        out_specs=vmem_spec(),
        compiler_params=pltpu.CompilerParams(vmem_limit_bytes=VMEM_LIMIT),
        name="finish",
        cost_estimate=cost(2),
    )(dmixed, weight, dhidden, x_own)


def spread_kernel(place_ref, gate_ref, up_ref, down_ref, weight_ref, gain_ref, *refs):
    out_in_ref, out_down_ref, sums_ref = refs[-3:]

    @pl.when(pl.program_id(0) == 0)
    def _():
        sums_ref[...] = jnp.zeros_like(sums_ref)

    gain = gain_ref[...]
    for q in range(4):
        near = 128 * (q + (1 - 2 * (q % 2)) * place_ref[1])
        for source_ref, start in ((gate_ref, 0), (up_ref, 512)):
            lanes = pl.ds(pl.multiple_of(start + near, 128), 128)
            raw = source_ref[q].astype(F32)
            out_in_ref[0, :, lanes] = raw * gain
            sums_ref[...] += raw * weight_ref[0, :, lanes].astype(F32)
        lanes = pl.ds(pl.multiple_of(near, 128), 128)
        out_down_ref[0, :, lanes] = down_ref[q].astype(F32)


def spread_experts(place, source, weight, gain, filled=()):
    def piece(start):
        return pl.BlockSpec((4, 64, 128), lambda e, place: (e // 5, 0, start + e % 5))

    def rows(width):
        return pl.BlockSpec((1, 64, width), lambda e, place: (e, place[0], 0))

    return pl.pallas_call(
        spread_kernel,
        grid_spec=pltpu.PrefetchScalarGridSpec(
            num_scalar_prefetch=1,
            grid=(10,),
            in_specs=[
                piece(0),
                piece(5),
                piece(10),
                rows(1024),
                pl.BlockSpec((64, 1), lambda e, place: (place[0], 0)),
            ]
            + [pl.BlockSpec(memory_space=pl.ANY)] * len(filled),
            out_specs=(
                rows(1024),
                rows(512),
                pl.BlockSpec((64, 128), lambda e, place: (place[0], 0)),
            ),
        ),
        out_shape=(
            jax.ShapeDtypeStruct((10, 128, 1024), F32),
            jax.ShapeDtypeStruct((10, 128, 512), F32),
            jax.ShapeDtypeStruct((128, 128), F32),
        ),
        input_output_aliases={6 + i: i for i in range(len(filled))},
        compiler_params=pltpu.CompilerParams(vmem_limit_bytes=VMEM_LIMIT),
        name="spread_experts",
        cost_estimate=cost(5),
    )(place, source, source, source, weight, gain, *filled)


def spread_attention_kernel(
    core_ref, own_ref, other_ref, weight_ref, gain_ref, qkv_ref, proj_ref, router_ref, sums_ref
):
    def write(source_ref, row):
        gain = gain_ref[row : row + 64]
        place = slice(row, row + 64)
        raw = [source_ref[j].astype(F32) for j in range(8)]
        query = jnp.concatenate([part[:, 0:128] for part in raw], axis=1)
        key = jnp.concatenate([part[:, 128:192] for part in raw], axis=1)
        value = jnp.concatenate([part[:, 192:256] for part in raw], axis=1)
        qkv = jnp.concatenate([query, key, value], axis=1)
        qkv_ref[place] = qkv * gain
        sums_ref[place] = jnp.sum(qkv * weight_ref[place].astype(F32), axis=-1, keepdims=True)
        router = raw[0][:, 384:512]
        for j in range(8):
            proj_ref[place, 128 * j : 128 * j + 128] = raw[j][:, 256:384]
            if j > 0:
                router = router + raw[j][:, 384:512]
        router_ref[place] = router

    @pl.when(core_ref[0] == 0)
    def _():
        write(own_ref, 0)
        write(other_ref, 64)

    @pl.when(core_ref[0] == 1)
    def _():
        write(other_ref, 0)
        write(own_ref, 64)


def spread_attention(core, own, other, weight, gain):
    return pl.pallas_call(
        spread_attention_kernel,
        out_shape=(
            jax.ShapeDtypeStruct((128, 2048), F32),
            jax.ShapeDtypeStruct((128, 1024), F32),
            jax.ShapeDtypeStruct((128, 128), F32),
            jax.ShapeDtypeStruct((128, 1), F32),
        ),
        in_specs=[pl.BlockSpec(memory_space=pltpu.SMEM)] + [vmem_spec()] * 4,
        out_specs=tuple([vmem_spec()] * 4),
        compiler_params=pltpu.CompilerParams(vmem_limit_bytes=VMEM_LIMIT),
        name="spread_attention",
        cost_estimate=cost(2),
    )(core, own, other, weight, gain)


def fold_cores(core, parts):
    split = parts.reshape(8, 2, 64, parts.shape[2])
    mine = jnp.where(core == 0, split[:, 0], split[:, 1])
    theirs = jnp.where(core == 0, split[:, 1], split[:, 0])
    return (mine.astype(F32) + swap_core(theirs).astype(F32)).astype(BF16)


def gather_weights(pair):
    return lax.all_gather(pair, "fsdp", axis=0, tiled=False, axis_index_groups=ALONG_Z)


def join_weights(core, x_lo, gathered):
    other = swap_core(gathered)
    low = jnp.where(core == 0, gathered, other)
    high = jnp.where(core == 0, other, gathered)
    joined = jnp.stack([low, high], axis=2)
    first = jnp.where(x_lo == 0, joined[:, 0], joined[:, 1])
    second = jnp.where(x_lo == 0, joined[:, 1], joined[:, 0])
    return jnp.stack([first, second]).reshape(1024, gathered.shape[3])


def scatter_experts(x_lo, parts):
    split = parts.reshape(2, 4, 64, parts.shape[2])
    mine = jnp.where(x_lo == 0, split[0], split[1])
    theirs = jnp.where(x_lo == 0, split[1], split[0])
    return lax.psum_scatter(
        jnp.stack([mine, theirs], axis=1).reshape(512, parts.shape[2]),
        "fsdp",
        scatter_dimension=0,
        tiled=True,
        axis_index_groups=ALONG_Z,
    )


def body(
    tokens,
    block_order,
    routes,
    attn_gain,
    qkv_weight,
    proj_weight,
    moe_gain,
    router_weight,
    expert_in,
    expert_down,
    cotangent,
):
    index = lax.axis_index("ctx")
    chip = index // 2
    core = index % 2
    x_hi = chip % 2
    x_lo = lax.axis_index("fsdp") // 4
    x_own = tokens.reshape(128, 1024)
    g_own = cotangent.reshape(128, 1024)
    gain_one = attn_gain.astype(F32)[:, None]
    gain_two = moe_gain.astype(F32)[:, None]

    qkv_turned = jnp.concatenate(
        [
            qkv_weight[:, 0:1024].reshape(128, 8, 128),
            qkv_weight[:, 1024:1536].reshape(128, 8, 64),
            qkv_weight[:, 1536:2048].reshape(128, 8, 64),
        ],
        axis=2,
    ).reshape(128, 2048)
    qkv_turned = (qkv_turned.astype(F32) * gain_one).astype(BF16)
    qkv_part = lax.dynamic_slice(qkv_turned, (0, 256 * chip), (128, 256))
    qkv_slice = gather_fsdp(qkv_part).reshape(1024, 256)

    proj_half = lax.dynamic_slice(proj_weight, (64 * core, 0), (64, 1024))
    first = 5 * (chip // 4)
    lane = 128 * (chip % 4)
    in_by_expert = expert_in.transpose(1, 0, 2)
    down_by_expert = expert_down.transpose(1, 0, 2)
    row = 64 * core

    def piece(source, offset):
        taken = lax.dynamic_slice(source, (first, row, offset + lane), (5, 64, 128))
        return taken.transpose(1, 0, 2).reshape(64, 640)

    router_half = lax.dynamic_slice(router_weight, (row, 0), (64, 10))
    gain_half = lax.dynamic_slice(gain_two, (row, 0), (64, 1))
    with_gain = jnp.concatenate(
        [piece(in_by_expert, 0), piece(in_by_expert, 512)]
        + [jnp.pad(router_half, ((0, 0), (0, 118)))],
        axis=1,
    )
    with_gain = (with_gain.astype(F32) * gain_half).astype(BF16)
    moe_half = jnp.concatenate([with_gain, piece(down_by_expert, 0), proj_half], axis=1)
    moe_other = lax.ppermute(moe_half, "fsdp", X_LO)
    qkv_half = lax.dynamic_slice(qkv_turned, (row, 0), (64, 2048))
    qkv_other = lax.ppermute(qkv_half, "fsdp", X_LO)
    qkv_slice, moe_pieces, x_copies = lax.optimization_barrier(
        (qkv_slice, jnp.stack([moe_half, moe_other]), copies(x_own))
    )
    moe_gathered = gather_weights(moe_pieces)
    x_all = exchange_ctx(x_copies).reshape(1024, 1024)

    routes_low = jnp.pad(routes.reshape(128, 8).astype(BF16), ((0, 0), (0, 120)))
    g_copies = copies(jnp.concatenate([g_own, routes_low], axis=1))
    x_all, g_copies = lax.optimization_barrier((x_all, g_copies))
    upstream = exchange_ctx(g_copies).reshape(1024, 1152)

    orders = block_order.reshape(8, 2)
    order_own = jnp.where(core == 0, orders[:, 0], orders[:, 1])
    order_other = jnp.where(core == 0, orders[:, 1], orders[:, 0])
    order = jnp.stack([order_own, order_other])
    within = jnp.arange(128, dtype=jnp.int32)
    placed = jnp.where(within[None, :] < 64, order_own[:, None], 31 - order_own[:, None])
    positions = (placed * 64 + within[None, :] % 64).reshape(1, 1024)
    frequency = THETA ** (-(jnp.arange(32, dtype=F32) * 2.0) / HEAD_DIM)
    angles = frequency[:, None] * positions.astype(F32)
    cos_table = jnp.cos(angles)
    sin_table = jnp.sin(angles)

    xh_one, query, key_value = project(
        x_all,
        qkv_slice,
        cos_table,
        sin_table,
    )
    attended, kv_rows, kv_cols = attend_forward(order, query, key_value, swap_core(key_value))

    attended, upstream, moe_gathered, qkv_pieces = lax.optimization_barrier(
        (attended, upstream, moe_gathered, jnp.stack([qkv_half, qkv_other]))
    )
    moe_full = join_weights(core, x_lo, moe_gathered)
    qkv_gathered = gather_weights(qkv_pieces)

    hidden, gates, xh_two, act_gated, dgate_up, packed = experts(
        first.reshape(1).astype(jnp.int32),
        x_all,
        gather_ctx(attended),
        moe_full,
        upstream,
    )
    packed, qkv_gathered = lax.optimization_barrier((packed, qkv_gathered))
    parts = exchange_ctx(packed.reshape(8, 128, 1152))

    down_slice = moe_full[:, 1408:2048]
    out_part = dot_nt(act_gated, down_slice).astype(BF16)
    in_grad = dot_tn(xh_two, dgate_up).astype(BF16)
    down_grad = dot_tn(upstream[:, 0:1024], act_gated).astype(BF16)
    moe_fold = fold_cores(
        core, jnp.concatenate([in_grad, down_grad], axis=1).reshape(8, 128, 1920)
    )
    proj_slice = lax.dynamic_slice(moe_full, (0, 2048 + 128 * chip), (1024, 128))
    parts, out_part, moe_fold, proj_slice = lax.optimization_barrier(
        (parts, out_part, moe_fold, proj_slice)
    )
    moe_sum = scatter_experts(x_lo, moe_fold).reshape(2, 64, 1920)
    moe_near = lax.ppermute(moe_sum[1], "fsdp", X_LO)

    own_rows = 128 * chip
    hidden_own = lax.dynamic_slice(hidden, (own_rows, 0), (128, 1024))
    dhidden, dbranch, dlogits, normal_two = middle(
        chip.reshape(1).astype(jnp.int32), parts, hidden, gates, upstream, moe_full
    )
    dbranch_all = gather_ctx(dbranch).reshape(1024, 1024)
    qkv_full = join_weights(core, x_lo, qkv_gathered)
    dbranch_all, out_part, qkv_full, moe_near = lax.optimization_barrier(
        (dbranch_all, out_part, qkv_full, moe_near)
    )
    moe_sum = (moe_sum[0].astype(F32) + moe_near.astype(F32)).astype(BF16)
    moe_pair = jnp.stack([moe_sum, lax.ppermute(moe_sum, "ctx", X_HI)])
    out_parts = exchange_ctx(out_part.reshape(8, 128, 1024))
    router_part = dot_tn(normal_two, dlogits).astype(BF16)
    proj_part = dot_tn(dbranch_all, attended).astype(BF16)

    dquery, dkv_own, dkv_other = attend_backward(
        order, query, kv_rows, kv_cols, dbranch_all, proj_slice
    )
    dkv_other, out_parts, moe_pair = lax.optimization_barrier((dkv_other, out_parts, moe_pair))
    moe_own = lax.all_gather(moe_pair, "ctx", axis=0, tiled=True, axis_index_groups=ALONG_Y)
    layer_out = (hidden_own + total(out_parts)).astype(BF16)
    dmixed, qkv_part_grad = turn(
        dquery, dkv_own, swap_core(dkv_other), cos_table, sin_table, xh_one
    )
    attn_fold = fold_cores(
        core,
        jnp.concatenate([qkv_part_grad, proj_part, router_part], axis=1).reshape(8, 128, 512),
    )
    attn_parts, layer_out = lax.optimization_barrier((exchange_fsdp(attn_fold), layer_out))
    attn_sum = total(attn_parts).astype(BF16).reshape(1, 256, 128)
    tail = exchange_ctx(
        jnp.concatenate([dmixed, jnp.broadcast_to(attn_sum, (8, 256, 128))], axis=1)
    )
    own_place = jnp.stack([core, x_hi]).astype(jnp.int32)
    other_place = jnp.stack([1 - core, x_hi]).astype(jnp.int32)
    filled = spread_experts(own_place, moe_own, in_by_expert, gain_two)
    tail, *filled = lax.optimization_barrier((tail, *filled))
    dmixed_own = tail[:, 0:256].reshape(2048, 128)
    attn_own = tail[:, 256:512].reshape(8, 64, 512)
    tokens_grad = finish(dmixed_own, qkv_full, dhidden, x_own)
    qkv_grad, proj_grad, router_raw, attn_gain_grad = spread_attention(
        core.reshape(1).astype(jnp.int32), attn_own, swap_core(attn_own), qkv_weight, gain_one
    )
    router_raw = router_raw[:, 0:10]
    attn_gain_grad = attn_gain_grad.reshape(128)
    in_grad, down_grad, gain_sums = spread_experts(
        other_place, swap_core(moe_own), in_by_expert, gain_two, tuple(filled)
    )
    expert_in_grad = in_grad.transpose(1, 0, 2)
    expert_down_grad = down_grad.transpose(1, 0, 2)
    router_grad = router_raw * gain_two
    moe_gain_grad = jnp.sum(gain_sums, axis=1) + jnp.sum(
        router_raw * router_weight.astype(F32), axis=1
    )
    return (
        layer_out.reshape(1, 128, 1024),
        tokens_grad.reshape(1, 128, 1024),
        attn_gain_grad,
        qkv_grad,
        proj_grad,
        moe_gain_grad,
        router_grad,
        expert_in_grad,
        expert_down_grad,
    )


def solution(mesh):
    in_specs = (
        P("fsdp", "ctx", None),
        P(),
        P("fsdp", "ctx", None),
        P("fsdp"),
        P("fsdp", None),
        P("fsdp", None),
        P("fsdp"),
        P("fsdp", None),
        P("fsdp", None, None),
        P("fsdp", None, None),
        P("fsdp", "ctx", None),
    )
    out_specs = (
        P("fsdp", "ctx", None),
        P("fsdp", "ctx", None),
        P("fsdp"),
        P("fsdp", None),
        P("fsdp", None),
        P("fsdp"),
        P("fsdp", None),
        P("fsdp", None, None),
        P("fsdp", None, None),
    )
    return jax.shard_map(body, mesh=mesh, in_specs=in_specs, out_specs=out_specs, check_vma=False)
```

```python
import math

import jax
import jax.numpy as jnp
from jax import lax
from jax.experimental import pallas as pl
from jax.experimental.pallas import tpu as pltpu
from jax.sharding import PartitionSpec as P

HEAD_DIM = 64
EPSILON = 1e-06
THETA = 10000.0
NEGATIVE = -1e30
BF16 = jnp.bfloat16
F32 = jnp.float32
VMEM_LIMIT = 32 * 1024 * 1024

GROUPS = [[2 * i + c for i in range(8)] for c in range(2)]
PAIRS = [(i, i ^ 1) for i in range(16)]
X_HI = [(i, i ^ 2) for i in range(16)]
X_LO = [(i, i ^ 4) for i in range(8)]
ALONG_Y = [[4 * y + i for y in range(4)] for i in range(4)]
ALONG_Z = [[4 * x + z for z in range(4)] for x in range(2)]


def exchange_ctx(parts):
    return lax.all_to_all(parts, "ctx", 0, 0, tiled=True, axis_index_groups=GROUPS)


def exchange_fsdp(parts):
    return lax.all_to_all(parts, "fsdp", 0, 0, tiled=True)


def copies(own):
    return jnp.broadcast_to(own[None], (8,) + own.shape)


def gather_ctx(own):
    return exchange_ctx(copies(own))


def gather_fsdp(own):
    return exchange_fsdp(copies(own))


def swap_core(own):
    return lax.ppermute(own, "ctx", PAIRS)


def total(parts):
    return jnp.sum(parts.astype(F32), axis=0)


def dot(left, right):
    return jnp.dot(left, right, preferred_element_type=F32)


def dot_tn(left, right):
    return lax.dot_general(left, right, (((0,), (0,)), ((), ())), preferred_element_type=F32)


def dot_nt(left, right):
    return lax.dot_general(left, right, (((1,), (1,)), ((), ())), preferred_element_type=F32)


def query_block(block, half):
    lo = 64 * half
    return jnp.concatenate([block[0:64, lo : lo + 64], block[64:128, lo : lo + 64]], axis=1)


def masked(scores, keys, position):
    rows = lax.broadcasted_iota(jnp.int32, (512, 128), 0) + (keys - 512)
    lanes = lax.broadcasted_iota(jnp.int32, (512, 128), 1) % 64 + position * 64
    tail = jnp.where(rows <= lanes, scores[keys - 512 :], NEGATIVE)
    if keys == 512:
        return tail
    return jnp.concatenate([scores[: keys - 512], tail], axis=0)


def attend_kernel(order_ref, query_ref, own_ref, other_ref, out_ref, rows_ref, cols_ref):
    for number, source_ref in enumerate((own_ref, other_ref)):
        source = source_ref[...].astype(F32).T.astype(BF16)
        for k in range(8):
            b = order_ref[number, k]
            low = pl.multiple_of(b * 64, 64)
            high = pl.multiple_of((31 - b) * 64, 64)
            rows_ref[pl.ds(low, 64), :] = source[128 * k : 128 * k + 64]
            rows_ref[pl.ds(high, 64), :] = source[128 * k + 64 : 128 * k + 128]
    cols_ref[...] = rows_ref[...].astype(F32).T.astype(BF16)
    blank = jnp.zeros((64, 128), BF16)

    def attend(block, half, position, keys):
        right = jnp.concatenate([query_block(block, half), blank], axis=0)
        scores = masked(dot(rows_ref[0:keys, :], right), keys, position)
        exponent = jnp.exp(scores - jnp.max(scores, axis=0, keepdims=True))
        share = 1.0 / jnp.sum(exponent, axis=0, keepdims=True)
        out = dot(cols_ref[64:128, 0:keys], exponent.astype(BF16)) * share
        out = out.T
        return jnp.concatenate([out[0:64], out[64:128]], axis=1).astype(BF16)

    def step(k, carry):
        start = pl.multiple_of(k * 128, 128)
        block = query_ref[:, pl.ds(start, 128)]
        b = order_ref[0, k]

        def both(low_keys, high_keys):
            out_ref[pl.ds(start, 64), :] = attend(block, 0, b, low_keys)
            out_ref[pl.ds(pl.multiple_of(start + 64, 64), 64), :] = attend(
                block, 1, 31 - b, high_keys
            )

        @pl.when(b < 8)
        def _():
            both(512, 2048)

        @pl.when(b >= 8)
        def _():
            both(1024, 1536)

        return carry

    lax.fori_loop(0, 8, step, 0)


def attend_forward(order, query, own, other):
    vmem = pl.BlockSpec(memory_space=pltpu.VMEM)
    return pl.pallas_call(
        attend_kernel,
        out_shape=(
            jax.ShapeDtypeStruct((1024, 128), BF16),
            jax.ShapeDtypeStruct((2048, 128), BF16),
            jax.ShapeDtypeStruct((128, 2048), BF16),
        ),
        in_specs=[pl.BlockSpec(memory_space=pltpu.SMEM), vmem, vmem, vmem],
        out_specs=(vmem, vmem, vmem),
        compiler_params=pltpu.CompilerParams(vmem_limit_bytes=VMEM_LIMIT),
        name="attend_forward",
        cost_estimate=cost(11),
    )(order, query, own, other)


def attend_back_kernel(
    order_ref, query_ref, rows_ref, cols_ref, branch_ref, proj_ref,
    dquery_ref, own_ref, other_ref, acc_ref, grad_ref,
):
    grad_ref[...] = dot(branch_ref[...], proj_ref[...]).astype(BF16)
    acc_ref[...] = jnp.zeros_like(acc_ref)
    blank = jnp.zeros((64, 128), BF16)
    blank_t = jnp.zeros((128, 64), BF16)

    def back(block, grads, half, position, keys):
        query = query_block(block, half)
        query_t = query.astype(F32).T.astype(BF16)
        rows = grads[64 * half : 64 * half + 64]
        grad_t = jnp.concatenate([rows[:, 0:64], rows[:, 64:128]], axis=0)
        grad = grad_t.astype(F32).T.astype(BF16)
        right = jnp.concatenate(
            [jnp.concatenate([query, blank], axis=1), jnp.concatenate([blank, grad], axis=1)],
            axis=0,
        )
        both = dot(rows_ref[0:keys, :], right)
        scores = masked(both[:, 0:128], keys, position)
        dprobs = both[:, 128:256]
        exponent = jnp.exp(scores - jnp.max(scores, axis=0, keepdims=True))
        probs = exponent * (1.0 / jnp.sum(exponent, axis=0, keepdims=True))
        weighted = probs * dprobs
        mean = jnp.sum(weighted, axis=0, keepdims=True)
        dscores = (weighted - probs * mean).astype(BF16)
        pair = jnp.concatenate([dscores, probs.astype(BF16)], axis=1)
        right_t = jnp.concatenate(
            [
                jnp.concatenate([query_t, blank_t], axis=1),
                jnp.concatenate([blank_t, grad_t], axis=1),
            ],
            axis=0,
        )
        acc_ref[0:keys, :] += dot(pair, right_t)
        return dot(cols_ref[0:64, 0:keys], dscores)

    def step(k, carry):
        start = pl.multiple_of(k * 128, 128)
        block = query_ref[:, pl.ds(start, 128)]
        grads = grad_ref[pl.ds(start, 128), :]
        b = order_ref[0, k]

        def both(low_keys, high_keys):
            low = back(block, grads, 0, b, low_keys)
            high = back(block, grads, 1, 31 - b, high_keys)
            dquery_ref[0:64, pl.ds(start, 128)] = jnp.concatenate(
                [low[:, 0:64], high[:, 0:64]], axis=1
            )
            dquery_ref[64:128, pl.ds(start, 128)] = jnp.concatenate(
                [low[:, 64:128], high[:, 64:128]], axis=1
            )

        @pl.when(b < 8)
        def _():
            both(512, 2048)

        @pl.when(b >= 8)
        def _():
            both(1024, 1536)

        return carry

    lax.fori_loop(0, 8, step, 0)
    for number, target_ref in enumerate((own_ref, other_ref)):
        for k in range(8):
            b = order_ref[number, k]
            low = acc_ref[pl.ds(pl.multiple_of(b * 64, 64), 64), :]
            high = acc_ref[pl.ds(pl.multiple_of((31 - b) * 64, 64), 64), :]
            block = jnp.concatenate([low, high], axis=0).T
            target_ref[:, 128 * k : 128 * k + 128] = block.astype(target_ref.dtype)


def attend_backward(order, query, rows, cols, branch, proj):
    vmem = pl.BlockSpec(memory_space=pltpu.VMEM)
    return pl.pallas_call(
        attend_back_kernel,
        out_shape=(
            jax.ShapeDtypeStruct((128, 1024), F32),
            jax.ShapeDtypeStruct((128, 1024), F32),
            jax.ShapeDtypeStruct((128, 1024), BF16),
        ),
        in_specs=[pl.BlockSpec(memory_space=pltpu.SMEM)] + [vmem] * 5,
        out_specs=(vmem, vmem, vmem),
        scratch_shapes=[pltpu.VMEM((2048, 128), F32), pltpu.VMEM((1024, 128), BF16)],
        compiler_params=pltpu.CompilerParams(vmem_limit_bytes=VMEM_LIMIT),
        name="attend_backward",
        cost_estimate=cost(21),
    )(order, query, rows, cols, branch, proj)


def rotate(first, second, cos_table, sin_table):
    return first * cos_table - second * sin_table, second * cos_table + first * sin_table


def cost(microseconds):
    return pl.CostEstimate(
        flops=int(microseconds * 1.1e9), bytes_accessed=int(microseconds * 3e6), transcendentals=0
    )


def vmem_spec():
    return pl.BlockSpec(memory_space=pltpu.VMEM)


def project_kernel(x_ref, weight_ref, cos_ref, sin_ref, normal_ref, query_ref, kv_ref):
    x = x_ref[...].astype(F32)
    rstd = lax.rsqrt(jnp.mean(x * x, axis=-1, keepdims=True) + EPSILON)
    normal = (x * rstd).astype(BF16)
    normal_ref[...] = normal
    mixed = dot(normal, weight_ref[...]).T
    cos_table = cos_ref[...]
    sin_table = sin_ref[...]
    scale = 1.0 / math.sqrt(HEAD_DIM)
    for h in range(3):
        low, high = rotate(
            mixed[64 * h : 64 * h + 32], mixed[64 * h + 32 : 64 * h + 64], cos_table, sin_table
        )
        turned = jnp.concatenate([low, high], axis=0).astype(BF16)
        if h < 2:
            query_ref[64 * h : 64 * h + 64] = (turned.astype(F32) * scale).astype(BF16)
        else:
            kv_ref[0:64] = turned
    kv_ref[64:128] = mixed[192:256].astype(BF16)


def project(x_all, weight, cos_table, sin_table):
    rows = pl.BlockSpec((256, 1024), lambda i: (i, 0))
    columns = pl.BlockSpec((128, 256), lambda i: (0, i))
    table = pl.BlockSpec((32, 256), lambda i: (0, i))
    return pl.pallas_call(
        project_kernel,
        grid=(4,),
        out_shape=(
            jax.ShapeDtypeStruct((1024, 1024), BF16),
            jax.ShapeDtypeStruct((128, 1024), BF16),
            jax.ShapeDtypeStruct((128, 1024), BF16),
        ),
        in_specs=[rows, pl.BlockSpec((1024, 256), lambda i: (0, 0)), table, table],
        out_specs=(rows, columns, columns),
        compiler_params=pltpu.CompilerParams(vmem_limit_bytes=VMEM_LIMIT),
        name="project",
        cost_estimate=cost(2),
    )(x_all, weight, cos_table, sin_table)


def experts_kernel(
    first_ref,
    x_ref,
    attended_ref,
    moe_ref,
    upstream_ref,
    hidden_ref,
    gates_ref,
    normal_ref,
    act_ref,
    dgate_up_ref,
    packed_ref,
):
    first = first_ref[0]
    attended = jnp.concatenate([attended_ref[j] for j in range(8)], axis=1)
    hidden = x_ref[...].astype(F32) + dot_nt(attended, moe_ref[:, 2048:3072])
    hidden_ref[...] = hidden
    rstd = lax.rsqrt(jnp.mean(hidden * hidden, axis=-1, keepdims=True) + EPSILON)
    normal = (hidden * rstd).astype(BF16)
    normal_ref[...] = normal
    lanes = lax.broadcasted_iota(jnp.int32, (256, 128), 1)
    named = upstream_ref[:, 1024:1152].astype(F32).astype(jnp.int32)
    chosen = lanes == named[:, 0:1]
    for k in range(1, 8):
        chosen = chosen | (lanes == named[:, k : k + 1])
    logits = dot(normal, moe_ref[:, 1280:1408])
    held = jnp.where(chosen, logits, NEGATIVE)
    raised = jnp.where(chosen, jnp.exp(held - jnp.max(held, axis=-1, keepdims=True)), 0.0)
    gates = raised / jnp.sum(raised, axis=-1, keepdims=True)
    gates_ref[...] = jnp.where(lanes == 64, rstd, gates)
    gate_up = dot(normal, moe_ref[:, 0:1280])
    spread = dot(upstream_ref[:, 0:1024], moe_ref[:, 1408:2048])
    dgates = jnp.zeros((256, 128), F32)
    dgate_all = []
    dup_all = []
    for c in range(5):
        gate_pre = gate_up[:, 128 * c : 128 * c + 128]
        up_pre = gate_up[:, 640 + 128 * c : 768 + 128 * c]
        back = spread[:, 128 * c : 128 * c + 128]
        weight = jnp.sum(jnp.where(lanes == first + c, gates, 0.0), axis=-1, keepdims=True)
        sigmoid = 1.0 / (1.0 + jnp.exp(-gate_pre))
        silu = gate_pre * sigmoid
        act = silu * up_pre
        act_ref[:, 128 * c : 128 * c + 128] = (weight * act).astype(BF16)
        dact = weight * back
        dgate_all.append(
            (dact * up_pre * sigmoid * (1.0 + gate_pre * (1.0 - sigmoid))).astype(BF16)
        )
        dup_all.append((dact * silu).astype(BF16))
        share = jnp.sum(act * back, axis=-1, keepdims=True)
        dgates = dgates + jnp.where((lanes % 64) == first + c, share, 0.0)
    dgate_up = jnp.concatenate(dgate_all + dup_all, axis=1)
    dgate_up_ref[...] = dgate_up
    packed_ref[:, 0:1024] = dot_nt(dgate_up, moe_ref[:, 0:1280]).astype(BF16)
    high = dgates.astype(BF16)
    low = (dgates - high.astype(F32)).astype(BF16)
    packed_ref[:, 1024:1152] = jnp.where(lanes < 64, high, low)


def experts(first, x_all, attended, moe, upstream):
    def rows(width):
        return pl.BlockSpec((256, width), lambda i: (i, 0))

    return pl.pallas_call(
        experts_kernel,
        grid=(4,),
        out_shape=(
            jax.ShapeDtypeStruct((1024, 1024), F32),
            jax.ShapeDtypeStruct((1024, 128), F32),
            jax.ShapeDtypeStruct((1024, 1024), BF16),
            jax.ShapeDtypeStruct((1024, 640), BF16),
            jax.ShapeDtypeStruct((1024, 1280), BF16),
            jax.ShapeDtypeStruct((1024, 1152), BF16),
        ),
        in_specs=[
            pl.BlockSpec(memory_space=pltpu.SMEM),
            rows(1024),
            pl.BlockSpec((8, 256, 128), lambda i: (0, i, 0)),
            pl.BlockSpec((1024, 3072), lambda i: (0, 0)),
            rows(1152),
        ],
        out_specs=(
            rows(1024),
            rows(128),
            rows(1024),
            rows(640),
            rows(1280),
            rows(1152),
        ),
        compiler_params=pltpu.CompilerParams(vmem_limit_bytes=VMEM_LIMIT),
        name="experts",
        cost_estimate=cost(16),
    )(first, x_all, attended, moe, upstream)


def middle_kernel(
    chip_ref, parts_ref, hidden_ref, gates_ref, upstream_ref, router_ref,
    dhidden_ref, dbranch_ref, dlogits_ref, normal_ref,
):
    summed = parts_ref[0].astype(F32)
    for k in range(1, 8):
        summed = summed + parts_ref[k].astype(F32)
    lanes = lax.broadcasted_iota(jnp.int32, (128, 128), 1)
    gates = jnp.where(lanes < 64, gates_ref[...], 0.0)
    rstd = gates_ref[:, 64:65]
    pair = summed[:, 1024:1152]
    dgates = jnp.where(lanes < 64, pair + pltpu.roll(pair, 64, 1), 0.0)
    dlogits = gates * (dgates - jnp.sum(gates * dgates, axis=-1, keepdims=True))
    dlogits = dlogits.astype(BF16)
    dlogits_ref[...] = dlogits
    scaled = summed[:, 0:1024] + dot_nt(dlogits, router_ref[...])
    normal = hidden_ref[...] * rstd
    normal_ref[...] = normal.astype(BF16)
    dhidden = upstream_ref[...].astype(F32) + rstd * (
        scaled - normal * jnp.mean(scaled * normal, axis=-1, keepdims=True)
    )
    dhidden_ref[...] = dhidden
    dbranch_ref[...] = dhidden.astype(BF16)


def middle(chip, parts, hidden, gates, upstream, moe):
    def own(width):
        return pl.BlockSpec((128, width), lambda i, chip: (chip[0], 0))

    def whole(*shape):
        return pl.BlockSpec(shape, lambda i, chip: (0,) * len(shape))

    return pl.pallas_call(
        middle_kernel,
        grid_spec=pltpu.PrefetchScalarGridSpec(
            num_scalar_prefetch=1,
            grid=(1,),
            in_specs=[
                whole(8, 128, 1152),
                own(1024),
                own(128),
                own(1024),
                pl.BlockSpec((1024, 128), lambda i, chip: (0, 10)),
            ],
            out_specs=(
                whole(128, 1024),
                whole(128, 1024),
                whole(128, 128),
                whole(128, 1024),
            ),
        ),
        out_shape=(
            jax.ShapeDtypeStruct((128, 1024), F32),
            jax.ShapeDtypeStruct((128, 1024), BF16),
            jax.ShapeDtypeStruct((128, 128), BF16),
            jax.ShapeDtypeStruct((128, 1024), BF16),
        ),
        compiler_params=pltpu.CompilerParams(vmem_limit_bytes=VMEM_LIMIT),
        name="middle",
        cost_estimate=cost(2),
    )(chip, parts, hidden, gates, upstream, moe)


def turn_kernel(
    query_ref, own_ref, other_ref, cos_ref, sin_ref, normal_ref, parts_ref, grad_ref
):
    kv = own_ref[...] + other_ref[...].astype(F32)
    cos_table = cos_ref[...]
    sin_table = -sin_ref[...]
    scale = 1.0 / math.sqrt(HEAD_DIM)
    turned = []
    for source in (query_ref[0:64] * scale, query_ref[64:128] * scale, kv[0:64]):
        turned += list(rotate(source[0:32], source[32:64], cos_table, sin_table))
    mixed = jnp.concatenate(turned + [kv[64:128]], axis=0).astype(BF16)
    for k in range(8):
        parts_ref[k] = mixed[:, 128 * k : 128 * k + 128]
    grad_ref[...] = dot(mixed, normal_ref[...]).T.astype(BF16)


def turn(query, own, other, cos_table, sin_table, normal):
    return pl.pallas_call(
        turn_kernel,
        out_shape=(
            jax.ShapeDtypeStruct((8, 256, 128), BF16),
            jax.ShapeDtypeStruct((1024, 256), BF16),
        ),
        in_specs=[vmem_spec()] * 6,
        out_specs=(vmem_spec(), vmem_spec()),
        compiler_params=pltpu.CompilerParams(vmem_limit_bytes=VMEM_LIMIT),
        name="turn",
        cost_estimate=cost(2),
    )(query, own, other, cos_table, sin_table, normal)


def finish_kernel(dmixed_ref, weight_ref, dhidden_ref, x_ref, out_ref):
    dmixed = dmixed_ref[...].astype(F32).T.astype(BF16)
    scaled = dot_nt(dmixed, weight_ref[...])
    x = x_ref[...].astype(F32)
    rstd = lax.rsqrt(jnp.mean(x * x, axis=-1, keepdims=True) + EPSILON)
    normal = x * rstd
    out_ref[...] = dhidden_ref[...] + rstd * (
        scaled - normal * jnp.mean(scaled * normal, axis=-1, keepdims=True)
    )


def finish(dmixed, weight, dhidden, x_own):
    return pl.pallas_call(
        finish_kernel,
        out_shape=jax.ShapeDtypeStruct((128, 1024), F32),
        in_specs=[vmem_spec()] * 4,
        out_specs=vmem_spec(),
        compiler_params=pltpu.CompilerParams(vmem_limit_bytes=VMEM_LIMIT),
        name="finish",
        cost_estimate=cost(2),
    )(dmixed, weight, dhidden, x_own)


def spread_kernel(place_ref, gate_ref, up_ref, down_ref, weight_ref, gain_ref, *refs):
    out_in_ref, out_down_ref, sums_ref = refs[-3:]

    @pl.when(pl.program_id(0) == 0)
    def _():
        sums_ref[...] = jnp.zeros_like(sums_ref)

    gain = gain_ref[...]
    for q in range(4):
        near = 128 * (q + (1 - 2 * (q % 2)) * place_ref[1])
        for source_ref, start in ((gate_ref, 0), (up_ref, 512)):
            lanes = pl.ds(pl.multiple_of(start + near, 128), 128)
            raw = source_ref[q].astype(F32)
            out_in_ref[0, :, lanes] = raw * gain
            sums_ref[...] += raw * weight_ref[0, :, lanes].astype(F32)
        lanes = pl.ds(pl.multiple_of(near, 128), 128)
        out_down_ref[0, :, lanes] = down_ref[q].astype(F32)


def spread_experts(place, source, weight, gain, filled=()):
    def piece(start):
        return pl.BlockSpec((4, 64, 128), lambda e, place: (e // 5, 0, start + e % 5))

    def rows(width):
        return pl.BlockSpec((1, 64, width), lambda e, place: (e, place[0], 0))

    return pl.pallas_call(
        spread_kernel,
        grid_spec=pltpu.PrefetchScalarGridSpec(
            num_scalar_prefetch=1,
            grid=(10,),
            in_specs=[
                piece(0),
                piece(5),
                piece(10),
                rows(1024),
                pl.BlockSpec((64, 1), lambda e, place: (place[0], 0)),
            ]
            + [pl.BlockSpec(memory_space=pl.ANY)] * len(filled),
            out_specs=(
                rows(1024),
                rows(512),
                pl.BlockSpec((64, 128), lambda e, place: (place[0], 0)),
            ),
        ),
        out_shape=(
            jax.ShapeDtypeStruct((10, 128, 1024), F32),
            jax.ShapeDtypeStruct((10, 128, 512), F32),
            jax.ShapeDtypeStruct((128, 128), F32),
        ),
        input_output_aliases={6 + i: i for i in range(len(filled))},
        compiler_params=pltpu.CompilerParams(vmem_limit_bytes=VMEM_LIMIT),
        name="spread_experts",
        cost_estimate=cost(5),
    )(place, source, source, source, weight, gain, *filled)


def spread_attention_kernel(
    core_ref, own_ref, other_ref, weight_ref, gain_ref, qkv_ref, proj_ref, router_ref, sums_ref
):
    def write(source_ref, row):
        gain = gain_ref[row : row + 64]
        place = slice(row, row + 64)
        raw = [source_ref[j].astype(F32) for j in range(8)]
        query = jnp.concatenate([part[:, 0:128] for part in raw], axis=1)
        key = jnp.concatenate([part[:, 128:192] for part in raw], axis=1)
        value = jnp.concatenate([part[:, 192:256] for part in raw], axis=1)
        qkv = jnp.concatenate([query, key, value], axis=1)
        qkv_ref[place] = qkv * gain
        sums_ref[place] = jnp.sum(qkv * weight_ref[place].astype(F32), axis=-1, keepdims=True)
        router = raw[0][:, 384:512]
        for j in range(8):
            proj_ref[place, 128 * j : 128 * j + 128] = raw[j][:, 256:384]
            if j > 0:
                router = router + raw[j][:, 384:512]
        router_ref[place] = router

    @pl.when(core_ref[0] == 0)
    def _():
        write(own_ref, 0)
        write(other_ref, 64)

    @pl.when(core_ref[0] == 1)
    def _():
        write(other_ref, 0)
        write(own_ref, 64)


def spread_attention(core, own, other, weight, gain):
    return pl.pallas_call(
        spread_attention_kernel,
        out_shape=(
            jax.ShapeDtypeStruct((128, 2048), F32),
            jax.ShapeDtypeStruct((128, 1024), F32),
            jax.ShapeDtypeStruct((128, 128), F32),
            jax.ShapeDtypeStruct((128, 1), F32),
        ),
        in_specs=[pl.BlockSpec(memory_space=pltpu.SMEM)] + [vmem_spec()] * 4,
        out_specs=tuple([vmem_spec()] * 4),
        compiler_params=pltpu.CompilerParams(vmem_limit_bytes=VMEM_LIMIT),
        name="spread_attention",
        cost_estimate=cost(2),
    )(core, own, other, weight, gain)


def fold_cores(core, parts):
    split = parts.reshape(8, 2, 64, parts.shape[2])
    mine = jnp.where(core == 0, split[:, 0], split[:, 1])
    theirs = jnp.where(core == 0, split[:, 1], split[:, 0])
    return (mine.astype(F32) + swap_core(theirs).astype(F32)).astype(BF16)


def gather_weights(pair):
    return lax.all_gather(pair, "fsdp", axis=0, tiled=False, axis_index_groups=ALONG_Z)


def join_weights(core, x_lo, gathered):
    other = swap_core(gathered)
    low = jnp.where(core == 0, gathered, other)
    high = jnp.where(core == 0, other, gathered)
    joined = jnp.stack([low, high], axis=2)
    first = jnp.where(x_lo == 0, joined[:, 0], joined[:, 1])
    second = jnp.where(x_lo == 0, joined[:, 1], joined[:, 0])
    return jnp.stack([first, second]).reshape(1024, gathered.shape[3])


def scatter_experts(x_lo, parts):
    split = parts.reshape(2, 4, 64, parts.shape[2])
    mine = jnp.where(x_lo == 0, split[0], split[1])
    theirs = jnp.where(x_lo == 0, split[1], split[0])
    return lax.psum_scatter(
        jnp.stack([mine, theirs], axis=1).reshape(512, parts.shape[2]),
        "fsdp",
        scatter_dimension=0,
        tiled=True,
        axis_index_groups=ALONG_Z,
    )


def body(
    tokens,
    block_order,
    routes,
    attn_gain,
    qkv_weight,
    proj_weight,
    moe_gain,
    router_weight,
    expert_in,
    expert_down,
    cotangent,
):
    index = lax.axis_index("ctx")
    chip = index // 2
    core = index % 2
    x_hi = chip % 2
    x_lo = lax.axis_index("fsdp") // 4
    x_own = tokens.reshape(128, 1024)
    g_own = cotangent.reshape(128, 1024)
    gain_one = attn_gain.astype(F32)[:, None]
    gain_two = moe_gain.astype(F32)[:, None]

    qkv_turned = jnp.concatenate(
        [
            qkv_weight[:, 0:1024].reshape(128, 8, 128),
            qkv_weight[:, 1024:1536].reshape(128, 8, 64),
            qkv_weight[:, 1536:2048].reshape(128, 8, 64),
        ],
        axis=2,
    ).reshape(128, 2048)
    qkv_turned = (qkv_turned.astype(F32) * gain_one).astype(BF16)
    qkv_part = lax.dynamic_slice(qkv_turned, (0, 256 * chip), (128, 256))
    qkv_slice = gather_fsdp(qkv_part).reshape(1024, 256)

    proj_half = lax.dynamic_slice(proj_weight, (64 * core, 0), (64, 1024))
    first = 5 * (chip // 4)
    lane = 128 * (chip % 4)
    in_by_expert = expert_in.transpose(1, 0, 2)
    down_by_expert = expert_down.transpose(1, 0, 2)
    row = 64 * core

    def piece(source, offset):
        taken = lax.dynamic_slice(source, (first, row, offset + lane), (5, 64, 128))
        return taken.transpose(1, 0, 2).reshape(64, 640)

    router_half = lax.dynamic_slice(router_weight, (row, 0), (64, 10))
    gain_half = lax.dynamic_slice(gain_two, (row, 0), (64, 1))
    with_gain = jnp.concatenate(
        [piece(in_by_expert, 0), piece(in_by_expert, 512)]
        + [jnp.pad(router_half, ((0, 0), (0, 118)))],
        axis=1,
    )
    with_gain = (with_gain.astype(F32) * gain_half).astype(BF16)
    moe_half = jnp.concatenate([with_gain, piece(down_by_expert, 0), proj_half], axis=1)
    moe_other = lax.ppermute(moe_half, "fsdp", X_LO)
    qkv_half = lax.dynamic_slice(qkv_turned, (row, 0), (64, 2048))
    qkv_other = lax.ppermute(qkv_half, "fsdp", X_LO)
    qkv_slice, moe_pieces, x_copies = lax.optimization_barrier(
        (qkv_slice, jnp.stack([moe_half, moe_other]), copies(x_own))
    )
    moe_gathered = gather_weights(moe_pieces)
    x_all = exchange_ctx(x_copies).reshape(1024, 1024)

    routes_low = jnp.pad(routes.reshape(128, 8).astype(BF16), ((0, 0), (0, 120)))
    g_copies = copies(jnp.concatenate([g_own, routes_low], axis=1))
    x_all, g_copies = lax.optimization_barrier((x_all, g_copies))
    upstream = exchange_ctx(g_copies).reshape(1024, 1152)

    orders = block_order.reshape(8, 2)
    order_own = jnp.where(core == 0, orders[:, 0], orders[:, 1])
    order_other = jnp.where(core == 0, orders[:, 1], orders[:, 0])
    order = jnp.stack([order_own, order_other])
    within = jnp.arange(128, dtype=jnp.int32)
    placed = jnp.where(within[None, :] < 64, order_own[:, None], 31 - order_own[:, None])
    positions = (placed * 64 + within[None, :] % 64).reshape(1, 1024)
    frequency = THETA ** (-(jnp.arange(32, dtype=F32) * 2.0) / HEAD_DIM)
    angles = frequency[:, None] * positions.astype(F32)
    cos_table = jnp.cos(angles)
    sin_table = jnp.sin(angles)

    xh_one, query, key_value = project(
        x_all,
        qkv_slice,
        cos_table,
        sin_table,
    )
    attended, kv_rows, kv_cols = attend_forward(order, query, key_value, swap_core(key_value))

    attended, upstream, moe_gathered, qkv_pieces = lax.optimization_barrier(
        (attended, upstream, moe_gathered, jnp.stack([qkv_half, qkv_other]))
    )
    moe_full = join_weights(core, x_lo, moe_gathered)
    qkv_gathered = gather_weights(qkv_pieces)

    hidden, gates, xh_two, act_gated, dgate_up, packed = experts(
        first.reshape(1).astype(jnp.int32),
        x_all,
        gather_ctx(attended),
        moe_full,
        upstream,
    )
    packed, qkv_gathered = lax.optimization_barrier((packed, qkv_gathered))
    parts = exchange_ctx(packed.reshape(8, 128, 1152))

    down_slice = moe_full[:, 1408:2048]
    out_part = dot_nt(act_gated, down_slice).astype(BF16)
    in_grad = dot_tn(xh_two, dgate_up).astype(BF16)
    down_grad = dot_tn(upstream[:, 0:1024], act_gated).astype(BF16)
    moe_fold = fold_cores(
        core, jnp.concatenate([in_grad, down_grad], axis=1).reshape(8, 128, 1920)
    )
    proj_slice = lax.dynamic_slice(moe_full, (0, 2048 + 128 * chip), (1024, 128))
    parts, out_part, moe_fold, proj_slice = lax.optimization_barrier(
        (parts, out_part, moe_fold, proj_slice)
    )
    moe_sum = scatter_experts(x_lo, moe_fold).reshape(2, 64, 1920)
    moe_near = lax.ppermute(moe_sum[1], "fsdp", X_LO)

    own_rows = 128 * chip
    hidden_own = lax.dynamic_slice(hidden, (own_rows, 0), (128, 1024))
    dhidden, dbranch, dlogits, normal_two = middle(
        chip.reshape(1).astype(jnp.int32), parts, hidden, gates, upstream, moe_full
    )
    dbranch_all = gather_ctx(dbranch).reshape(1024, 1024)
    qkv_full = join_weights(core, x_lo, qkv_gathered)
    dbranch_all, out_part, qkv_full, moe_near = lax.optimization_barrier(
        (dbranch_all, out_part, qkv_full, moe_near)
    )
    moe_sum = (moe_sum[0].astype(F32) + moe_near.astype(F32)).astype(BF16)
    moe_pair = jnp.stack([moe_sum, lax.ppermute(moe_sum, "ctx", X_HI)])
    out_parts = exchange_ctx(out_part.reshape(8, 128, 1024))
    router_part = dot_tn(normal_two, dlogits).astype(BF16)
    proj_part = dot_tn(dbranch_all, attended).astype(BF16)

    dquery, dkv_own, dkv_other = attend_backward(
        order, query, kv_rows, kv_cols, dbranch_all, proj_slice
    )
    dkv_other, out_parts, moe_pair = lax.optimization_barrier((dkv_other, out_parts, moe_pair))
    moe_own = lax.all_gather(moe_pair, "ctx", axis=0, tiled=True, axis_index_groups=ALONG_Y)
    layer_out = (hidden_own + total(out_parts)).astype(BF16)
    dmixed, qkv_part_grad = turn(
        dquery, dkv_own, swap_core(dkv_other), cos_table, sin_table, xh_one
    )
    attn_fold = fold_cores(
        core,
        jnp.concatenate([qkv_part_grad, proj_part, router_part], axis=1).reshape(8, 128, 512),
    )
    attn_parts, layer_out = lax.optimization_barrier((exchange_fsdp(attn_fold), layer_out))
    attn_sum = total(attn_parts).astype(BF16).reshape(1, 256, 128)
    tail = exchange_ctx(
        jnp.concatenate([dmixed, jnp.broadcast_to(attn_sum, (8, 256, 128))], axis=1)
    )
    own_place = jnp.stack([core, x_hi]).astype(jnp.int32)
    other_place = jnp.stack([1 - core, x_hi]).astype(jnp.int32)
    filled = spread_experts(own_place, moe_own, in_by_expert, gain_two)
    tail, *filled = lax.optimization_barrier((tail, *filled))
    dmixed_own = tail[:, 0:256].reshape(2048, 128)
    attn_own = tail[:, 256:512].reshape(8, 64, 512)
    tokens_grad = finish(dmixed_own, qkv_full, dhidden, x_own)
    qkv_grad, proj_grad, router_raw, attn_gain_grad = spread_attention(
        core.reshape(1).astype(jnp.int32), attn_own, swap_core(attn_own), qkv_weight, gain_one
    )
    router_raw = router_raw[:, 0:10]
    attn_gain_grad = attn_gain_grad.reshape(128)
    in_grad, down_grad, gain_sums = spread_experts(
        other_place, swap_core(moe_own), in_by_expert, gain_two, tuple(filled)
    )
    expert_in_grad = in_grad.transpose(1, 0, 2)
    expert_down_grad = down_grad.transpose(1, 0, 2)
    router_grad = router_raw * gain_two
    moe_gain_grad = jnp.sum(gain_sums, axis=1) + jnp.sum(
        router_raw * router_weight.astype(F32), axis=1
    )
    return (
        layer_out.reshape(1, 128, 1024),
        tokens_grad.reshape(1, 128, 1024),
        attn_gain_grad,
        qkv_grad,
        proj_grad,
        moe_gain_grad,
        router_grad,
        expert_in_grad,
        expert_down_grad,
    )


def solution(mesh):
    in_specs = (
        P("fsdp", "ctx", None),
        P(),
        P("fsdp", "ctx", None),
        P("fsdp"),
        P("fsdp", None),
        P("fsdp", None),
        P("fsdp"),
        P("fsdp", None),
        P("fsdp", None, None),
        P("fsdp", None, None),
        P("fsdp", "ctx", None),
    )
    out_specs = (
        P("fsdp", "ctx", None),
        P("fsdp", "ctx", None),
        P("fsdp"),
        P("fsdp", None),
        P("fsdp", None),
        P("fsdp"),
        P("fsdp", None),
        P("fsdp", None, None),
        P("fsdp", None, None),
    )
    return jax.shard_map(body, mesh=mesh, in_specs=in_specs, out_specs=out_specs, check_vma=False)
```
